128 devices in a mesh: frame: 8 (over z, y_hi), token: 8 (over x, y_lo), batch: 2 (over core).
Axes of the slice: x: 4, y: 4 (y_hi: 2, y_lo: 2; y = y_hi * 2 + y_lo), z: 4, core: 2. Of those that a mesh axis runs over, the one named last changes fastest.
Arguments:
- encoder_out: bfloat16 [2, 512, 512], P('batch', 'frame', 'token'), may hold values from -6 to 6
- predictor_out: bfloat16 [2, 512, 512], P('batch', 'token', 'frame'), may hold values from -6 to 6
- enc_weight: bfloat16 [512, 512], replicated, may hold values from -0.25 to 0.25
- pred_weight: bfloat16 [512, 512], replicated, may hold values from -0.25 to 0.25
- joint_bias: float32 [512], replicated, may hold values from -0.5 to 0.5
- out_weight: bfloat16 [512, 1024], replicated, may hold values from -0.076171875 to 0.076171875
- blank_occupancy: float32 [2, 512, 512], P('batch', 'frame', 'token'), may hold values from 0.05 to 1
- label_occupancy: float32 [2, 512, 512], P('batch', 'frame', 'token'), may hold values from 0.05 to 1
- frame_lengths: int32 [2], replicated, may hold values from 64 to 512, as said below
- token_lengths: int32 [2], replicated, may hold values from 64 to 511, as said below
- target_ids: int32 [2, 512], P(None, 'token'), may hold values from 1 to 1023
Outputs:
- enc_grad: float32 [2, 512, 512], P('batch', 'frame', 'token')
- pred_grad: float32 [2, 512, 512], P('batch', 'token', 'frame')
- enc_weight_grad: float32 [512, 512], P(('frame', 'token', 'batch'))
- pred_weight_grad: float32 [512, 512], P(('frame', 'token', 'batch'))
- out_weight_grad: float32 [512, 1024], P(('frame', 'token', 'batch'))
- bias_grad: float32 [512], P(('frame', 'token', 'batch'))
The draws below stay inside these ranges and needn't reach their ends.
Inputs may be any that keep to these rules, and one draw needn't show every extreme that they name: `frame_lengths`: frames of each utterance; in every draw some utterance has all 512. `token_lengths`: target tokens of each utterance; in every draw some utterance has 511. `target_ids`: entry 0 is the blank and is never a target.
All inputs are finite; a program needn't handle non-finite values.
Results may differ from the reference program's by a relative error of at most 0.00059.
Values may be sent and summed in bfloat16 or wider, within the bound.
No kernel may reach another device: no remote copies, remote signals or barrier semaphores. Data moves between devices by JAX's collectives and lax.ppermute only.
A program may use at most 64 MiB of HBM per device.

```python
import math
import jax
import jax.numpy as jnp
from jax import lax

D = 512
J = 512
V = 1024
FB = 8
FRAMES = 512
POSITIONS = 512
UTTS = 2


def draw_frame_lengths(key, part):
    key = jax.random.fold_in(key, 11)
    first_key, second_key = jax.random.split(key)
    drawn = jax.random.randint(first_key, (UTTS,), FRAMES // 8, FRAMES + 1)
    longest = jax.random.randint(second_key, (), 0, UTTS)
    return jnp.where(jnp.arange(UTTS) == longest, FRAMES, drawn).astype(jnp.int32)


def draw_token_lengths(key, part):
    key = jax.random.fold_in(key, 23)
    first_key, second_key = jax.random.split(key)
    drawn = jax.random.randint(first_key, (UTTS,), POSITIONS // 8, POSITIONS)
    longest = jax.random.randint(second_key, (), 0, UTTS)
    return jnp.where(jnp.arange(UTTS) == longest, POSITIONS - 1, drawn).astype(jnp.int32)


def set_ends(values, rng, least, largest):
    extent = values.shape
    index_at = [jax.random.randint(jax.random.fold_in(rng, axis), (), 0, extent[axis]) for axis in range(len(extent))]
    values = values.at[tuple(index_at)].set(least)
    longest = extent.index(max(extent))
    index_at[longest] = (index_at[longest] + 1) % extent[longest]
    return values.at[tuple(index_at)].set(largest)


def levels(own_key, extent, cuts, low, high):
    loudness, own = 1.0, jax.random.fold_in(own_key, 6)
    for dim, parts in cuts:
        steps = jnp.exp(jax.random.uniform(jax.random.fold_in(own, dim), (parts,), jnp.float32, low / len(cuts), high / len(cuts)))
        loudness = loudness * jnp.repeat(steps, extent[dim] // parts).reshape([-1 if axis == dim else 1 for axis in range(len(extent))])
    return loudness


def centred(stream_key, dims, scale, bound, cuts=(), kind=jnp.bfloat16):
    values = scale * jax.random.normal(stream_key, dims, jnp.float32)
    if cuts:
        values = values * levels(stream_key, dims, cuts, -0.22, 0.18)
    return jnp.clip(values, -bound, bound).astype(kind)


def setup_inputs(seed: int = 0) -> dict:
    streams_of = jax.random.split(jax.random.key(seed), 12)
    encoder_out = centred(streams_of[0], (UTTS, FRAMES, D), 1.0, 6.0, ((0, 2), (1, 8), (2, 8)))
    predictor_out = centred(streams_of[1], (UTTS, POSITIONS, D), 1.0, 6.0, ((0, 2), (1, 8), (2, 8)))
    enc_weight = centred(streams_of[2], (D, J), D ** -0.5, 0.25)
    pred_weight = centred(streams_of[3], (D, J), D ** -0.5, 0.25)
    joint_bias = jnp.clip(jax.random.uniform(streams_of[4], (J,), jnp.float32, -0.5, 0.5), -0.5, 0.5)
    out_weight = jnp.clip(jax.random.uniform(streams_of[5], (J, V), jnp.float32, -0.076171875, 0.076171875), -0.076171875, 0.076171875).astype(jnp.bfloat16)
    blank_occupancy = jnp.clip(jnp.exp(math.log(1.0) - 2.9957323 * jax.random.uniform(streams_of[6], (UTTS, FRAMES, POSITIONS), jnp.float32) ** levels(streams_of[6], (UTTS, FRAMES, POSITIONS), ((0, 2), (1, 8), (2, 8)), -0.2, 0.2)), 0.05, 1.0)
    label_occupancy = jnp.clip(jnp.exp(math.log(1.0) - 2.9957323 * jax.random.uniform(streams_of[7], (UTTS, FRAMES, POSITIONS), jnp.float32) ** levels(streams_of[7], (UTTS, FRAMES, POSITIONS), ((0, 2), (1, 8), (2, 8)), -0.2, 0.2)), 0.05, 1.0)
    frame_lengths = draw_frame_lengths(jax.random.fold_in(streams_of[11], 71), 0)
    token_lengths = draw_token_lengths(jax.random.fold_in(streams_of[11], 71), 0)
    target_ids = set_ends(jax.random.randint(streams_of[10], (UTTS, POSITIONS), 1, V), jax.random.fold_in(streams_of[10], 1), 1, V - 1).astype(jnp.int32)
    return {"encoder_out": encoder_out, "predictor_out": predictor_out, "enc_weight": enc_weight, "pred_weight": pred_weight, "joint_bias": joint_bias, "out_weight": out_weight, "blank_occupancy": blank_occupancy, "label_occupancy": label_occupancy, "frame_lengths": frame_lengths, "token_lengths": token_lengths, "target_ids": target_ids}


def cell_hidden(frame_rows, pred_rows, joint_bias):
    inner = frame_rows[:, None, :] + pred_rows[None, :, :] + joint_bias
    return jnp.tanh(inner).astype(jnp.bfloat16).reshape(-1, inner.shape[2])

def cell_weights(blanks, labels, first_frame, first_token, frame_len, token_len):
    frame_pos = first_frame + jnp.arange(blanks.shape[0], dtype=jnp.int32)
    token_pos = first_token + jnp.arange(blanks.shape[1], dtype=jnp.int32)
    active_frame = (frame_pos < frame_len)[:, None]
    blank_weight = jnp.where(active_frame & (token_pos <= token_len)[None, :], blanks, 0.0)
    label_weight = jnp.where(active_frame & (token_pos < token_len)[None, :], labels, 0.0)
    return (blank_weight.reshape(-1), label_weight.reshape(-1))

def logit_grad(logits, log_total, blank_weight, label_weight, cell_targets, first_vocab):
    prob = jnp.exp(logits - log_total[:, None])
    vocab = first_vocab + jnp.arange(logits.shape[1], dtype=jnp.int32)
    grad = (blank_weight + label_weight)[:, None] * prob
    grad = grad - jnp.where(vocab[None, :] == 0, blank_weight[:, None], 0.0)
    grad = grad - jnp.where(vocab[None, :] == cell_targets[:, None], label_weight[:, None], 0.0)
    return grad.astype(jnp.bfloat16)

def cell_backward(hidden, grad_hidden):
    hidden_full = hidden.astype(jnp.float32)
    return grad_hidden * (1.0 - hidden_full * hidden_full)

def contract_rows(left, right):
    return lax.dot_general(left, right, (((0,), (0,)), ((), ())), preferred_element_type=jnp.float32)

def contract_cols(left, right):
    return lax.dot_general(left, right, (((1,), (1,)), ((), ())), preferred_element_type=jnp.float32)

def reference(encoder_out, predictor_out, enc_weight, pred_weight, joint_bias, out_weight, blank_occupancy, label_occupancy, frame_lengths, token_lengths, target_ids):
    enc_list = []
    pred_list = []
    enc_wgrad = jnp.zeros((D, J), jnp.float32)
    pred_wgrad = jnp.zeros((D, J), jnp.float32)
    out_wgrad = jnp.zeros((J, V), jnp.float32)
    bias_total = jnp.zeros((J,), jnp.float32)
    for utterance in range(UTTS):
        enc_proj = jnp.dot(encoder_out[utterance], enc_weight, preferred_element_type=jnp.float32)
        pred_proj = jnp.dot(predictor_out[utterance], pred_weight, preferred_element_type=jnp.float32)
        frame_len = frame_lengths[utterance]
        token_len = token_lengths[utterance]
        cell_targets = jnp.tile(target_ids[utterance], FB)
        blank_all = blank_occupancy[utterance]
        label_all = label_occupancy[utterance]

        def frame_step(totals, block_index, enc_proj=enc_proj, pred_proj=pred_proj, frame_len=frame_len, token_len=token_len, cell_targets=cell_targets, blank_all=blank_all, label_all=label_all):
            grad_pred, grad_bias, grad_out = totals
            first_row = block_index * FB
            frame_rows = lax.dynamic_slice_in_dim(enc_proj, first_row, FB, 0)
            blanks = lax.dynamic_slice_in_dim(blank_all, first_row, FB, 0)
            labels = lax.dynamic_slice_in_dim(label_all, first_row, FB, 0)
            hidden = cell_hidden(frame_rows, pred_proj, joint_bias)
            blank_weight, label_weight = cell_weights(blanks, labels, first_row, jnp.int32(0), frame_len, token_len)
            logits = jnp.dot(hidden, out_weight, preferred_element_type=jnp.float32)
            log_total = jnp.log(lax.optimization_barrier(jnp.sum(jnp.exp(logits), axis=1)))
            grad_logits = logit_grad(logits, log_total, blank_weight, label_weight, cell_targets, jnp.int32(0))
            grad_hidden = contract_cols(grad_logits, out_weight)
            grad_inner = cell_backward(hidden, grad_hidden).reshape(FB, POSITIONS, J)
            grad_out = grad_out + contract_rows(hidden, grad_logits)
            return ((grad_pred + grad_inner.sum(0), grad_bias + grad_inner.sum((0, 1)), grad_out), grad_inner.sum(1))
        start = (jnp.zeros((POSITIONS, J), jnp.float32), jnp.zeros((J,), jnp.float32), jnp.zeros((J, V), jnp.float32))
        (grad_pred, grad_bias, grad_out), grad_rows = lax.scan(frame_step, start, jnp.arange(FRAMES // FB, dtype=jnp.int32))
        grad_rows = grad_rows.reshape(FRAMES, J)
        enc_list.append(jnp.dot(grad_rows, enc_weight.astype(jnp.float32).T, precision=lax.Precision.HIGHEST))
        pred_list.append(jnp.dot(grad_pred, pred_weight.astype(jnp.float32).T, precision=lax.Precision.HIGHEST))
        enc_wgrad = enc_wgrad + jnp.dot(encoder_out[utterance].astype(jnp.float32).T, grad_rows, precision=lax.Precision.HIGHEST)
        pred_wgrad = pred_wgrad + jnp.dot(predictor_out[utterance].astype(jnp.float32).T, grad_pred, precision=lax.Precision.HIGHEST)
        out_wgrad = out_wgrad + grad_out
        bias_total = bias_total + grad_bias
    return (jnp.stack(enc_list), jnp.stack(pred_list), enc_wgrad, pred_wgrad, out_wgrad, bias_total)
```

```python
import jax
import jax.numpy as jnp
from jax import lax
from jax.experimental import pallas as pl
from jax.experimental.pallas import tpu as pltpu
from jax.sharding import PartitionSpec as P

FB = 16
CHUNK = 256
BIG = 63 * 1024 * 1024
ALL = ("frame", "token", "batch")
F32, BF16 = jnp.float32, jnp.bfloat16


def split3(x):
    hi = x.astype(BF16)
    rest = x - hi.astype(F32)
    mid = rest.astype(BF16)
    lo = (rest - mid.astype(F32)).astype(BF16)
    return hi, mid, lo


def dot_nt(a, b):
    return lax.dot_general(a, b, (((1,), (1,)), ((), ())), preferred_element_type=F32)


def dot_tn(a, b):
    return lax.dot_general(a, b, (((0,), (0,)), ((), ())), preferred_element_type=F32)


def exact_nt(a, b):
    return sum(dot_nt(piece, b) for piece in split3(a))


def exact_tn(a, b):
    return sum(dot_tn(a, piece) for piece in split3(b))


def cells_kernel(
    g_hbm, h_hbm, encw_hbm, predw_hbm, bias_hbm, blank_hbm, label_hbm, tgt_hbm, flen_hbm, tlen_hbm, ow_hbm,
    keep_ref, send_ref, stash_hbm,
    g_ref, h_ref, encw_ref, predw_ref, bias_ref, blank_ref, label_ref, tgt_ref, flen_ref, tlen_ref, ow_ref,
    sems, out_sems, encp_ref, predp_ref, rows_ref, prow_ref, bw_ref, lw_ref, tgt_col_ref, e_ref, stash_ref,
):
    nf, nt = blank_ref.shape[1], blank_ref.shape[2]
    joint, vocab = ow_ref.shape
    parts, width = g_ref.shape[0], g_ref.shape[2] // 2
    cells = FB * nt
    core = lax.axis_index("batch")
    first = core == 0
    hbm = [g_hbm, h_hbm, encw_hbm, predw_hbm, bias_hbm, blank_hbm, label_hbm, tgt_hbm, flen_hbm, tlen_hbm, ow_hbm]
    here = [g_ref, h_ref, encw_ref, predw_ref, bias_ref, blank_ref, label_ref, tgt_ref, flen_ref, tlen_ref, ow_ref]
    copies = [pltpu.make_async_copy(src, dst, sems.at[i]) for i, (src, dst) in enumerate(zip(hbm, here))]
    for copy in copies:
        copy.start()
    for copy in copies[:-1]:
        copy.wait()
    frame_len = flen_ref[core]
    token_len = tlen_ref[core]
    first_frame = lax.axis_index("frame") * nf
    first_token = lax.axis_index("token") * nt

    encp = jnp.zeros((nf, joint), F32)
    predp = jnp.zeros((nt, joint), F32)
    for s in range(parts):
        own = g_ref[s][:, :width]
        other = h_ref[s][:, width:]
        rows = slice(s * width, (s + 1) * width)
        encp += jnp.dot(jnp.where(first, own, other), encw_ref[rows, :], preferred_element_type=F32)
        predp += jnp.dot(jnp.where(first, other, own), predw_ref[rows, :], preferred_element_type=F32)
    encp_ref[...] = encp
    predp_ref[...] = predp + bias_ref[...]

    frame_pos = first_frame + lax.broadcasted_iota(jnp.int32, (nf, nt), 0)
    token_pos = first_token + lax.broadcasted_iota(jnp.int32, (nf, nt), 1)
    live = frame_pos < frame_len
    bw_ref[...] = jnp.where(live & (token_pos <= token_len), blank_ref[0], 0.0)
    lw_ref[...] = jnp.where(live & (token_pos < token_len), label_ref[0], 0.0)
    diag = lax.broadcasted_iota(jnp.int32, (nt, nt), 0) == lax.broadcasted_iota(jnp.int32, (nt, nt), 1)
    targets = jnp.where(first, tgt_ref[0:1, :], tgt_ref[1:2, :]).astype(F32)
    tgt_col = jnp.sum(jnp.where(diag, targets, 0.0), axis=1, keepdims=True).astype(jnp.int32)
    tgt_col_ref[...] = jnp.broadcast_to(tgt_col, (nt, 128))
    prow_ref[...] = jnp.zeros_like(prow_ref)
    lane = lax.broadcasted_iota(jnp.int32, (FB, nt, 128), 2)
    copies[-1].wait()

    def columns(ref, t0):
        rows = ref[pl.ds(t0, FB), :]
        return jnp.sum(jnp.where(diag[None], rows[:, None, :], 0.0), axis=2, keepdims=True)

    def block(i, carry):
        t0 = pl.multiple_of(i * FB, FB)
        span = pl.ds(pl.multiple_of(i * cells, cells), cells)
        frames = encp_ref[pl.ds(t0, FB), :]
        inner = frames[:, None, :] + predp_ref[...][None, :, :]
        hidden = jnp.tanh(inner).astype(BF16).reshape(cells, joint)
        stash_ref[span, :joint] = hidden
        total = jnp.zeros((cells, 128), F32)
        for c in range(vocab // CHUNK):
            cols = slice(c * CHUNK, (c + 1) * CHUNK)
            e = jnp.exp(jnp.dot(hidden, ow_ref[:, cols], preferred_element_type=F32))
            e_ref[:, cols] = e
            for q in range(CHUNK // 128):
                total = total + e[:, q * 128 : (q + 1) * 128]
        total = jnp.sum(total, axis=1, keepdims=True).reshape(FB, nt, 1)
        bw = columns(bw_ref, t0)
        lw = columns(lw_ref, t0)
        scale = (bw + lw) / total
        tgt = tgt_col_ref[...][None]
        for v in range(vocab // 128):
            cols = slice(v * 128, (v + 1) * 128)
            g = e_ref[:, cols].reshape(FB, nt, 128) * scale
            if v == 0:
                g = g - jnp.where(lane == 0, bw, 0.0)
            g = g - jnp.where(lane == tgt - v * 128, lw, 0.0)
            stash_ref[span, joint + v * 128 : joint + (v + 1) * 128] = g.astype(BF16).reshape(cells, 128)
        pltpu.make_async_copy(stash_ref.at[span], stash_hbm.at[span], out_sems.at[i]).start()
        for c in range(joint // CHUNK):
            cols = slice(c * CHUNK, (c + 1) * CHUNK)
            grad_hidden = dot_nt(stash_ref[span, joint:], ow_ref[cols, :])
            hf = stash_ref[span, cols].astype(F32)
            gi = (grad_hidden * (1.0 - hf * hf)).reshape(FB, nt, CHUNK)
            prow_ref[:, cols] += gi.sum(0)
            rows_ref[pl.ds(t0, FB), cols] = gi.sum(1)
        return carry

    lax.fori_loop(0, nf // FB, block, 0)

    term_e = exact_nt(rows_ref[...], encw_ref[...])
    term_p = exact_nt(prow_ref[...], predw_ref[...])
    for s in range(parts):
        cols = slice(s * width, (s + 1) * width)
        e_part = jnp.concatenate([term_e[:, cols], rows_ref[:, cols]], axis=1)
        p_part = jnp.concatenate([term_p[:, cols], prow_ref[:, cols]], axis=1)
        keep_ref[s] = jnp.where(first, e_part, p_part)
        send_ref[s] = jnp.where(first, p_part, e_part)
    for i in range(nf // FB):
        span = pl.ds(i * cells, cells)
        pltpu.make_async_copy(stash_ref.at[span], stash_hbm.at[span], out_sems.at[i]).wait()


def wgrad_kernel(stash_hbm, g_ref, h_ref, keep_ref, send_ref, feat_ref, stash_ref, acc_ref, sems):
    parts, nt, two = g_ref.shape
    width = two // 2
    joint, vocab = acc_ref.shape
    first = lax.axis_index("batch") == 0
    steps = sems.shape[0]
    step = stash_ref.shape[0] // steps
    for i in range(steps):
        span = pl.ds(i * step, step)
        pltpu.make_async_copy(stash_hbm.at[span], stash_ref.at[span], sems.at[i]).start()
    for s in range(parts):
        for is_enc in (True, False):
            x = jnp.where(first == is_enc, g_ref[s], h_ref[s]).astype(F32)
            feat_ref[0 if is_enc else 1, s * width : (s + 1) * width, :] = jnp.concatenate(
                [x[:, :width].T, x[:, width:].T], axis=1
            ).astype(BF16)
    acc_ref[...] = jnp.zeros_like(acc_ref)

    def block(i, carry):
        span = pl.ds(pl.multiple_of(i * step, step), step)
        pltpu.make_async_copy(stash_hbm.at[span], stash_ref.at[span], sems.at[i]).wait()
        acc_ref[...] += dot_tn(stash_ref[span, :joint], stash_ref[span, joint:])
        return carry

    lax.fori_loop(0, steps, block, 0)

    chips = joint // 8
    top = lax.broadcasted_iota(jnp.int32, (chips, 8, 128), 1) < 4
    for v in range(vocab // 256):
        a = acc_ref[:, v * 256 : v * 256 + 128].reshape(chips, 8, 128)
        b = acc_ref[:, v * 256 + 128 : v * 256 + 256].reshape(chips, 8, 128)
        upper = jnp.where(top, a, pltpu.roll(b, 4, 1))
        lower = jnp.where(top, pltpu.roll(a, 4, 1), b)
        rows = slice(v * 8, v * 8 + 8)
        keep_ref[:, rows, :] = jnp.where(first, upper, lower)
        send_ref[:, rows, :] = jnp.where(first, lower, upper)


LEVELS = 32000.0
STEPS = 16.0


def pack_kernel(keep_ref, recv_ref, own_ref, partner_ref, feat_ref, out_ref, small_ref):
    chips, rows, _ = keep_ref.shape
    two = own_ref.shape[1]
    width = two // 2
    core = lax.axis_index("batch")
    first = core == 0
    own, partner = own_ref[:, width:], partner_ref[:, width:]
    enc_rows = jnp.where(first, own, partner)
    pred_rows = jnp.where(first, partner, own)
    parts = []
    for i, value in enumerate((enc_rows, pred_rows)):
        parts.append(sum(jnp.dot(feat_ref[i], piece, preferred_element_type=F32) for piece in split3(value)))
    weights = jnp.concatenate(parts, axis=1).reshape(chips, 8, two)
    weights = jnp.where(first, weights, pltpu.roll(weights, 4, 1))
    bias = jnp.sum(enc_rows, axis=0, keepdims=True)
    bias = jnp.concatenate([bias, jnp.zeros_like(bias)], axis=1)[None]
    sub = lax.broadcasted_iota(jnp.int32, (chips, 8, two), 1)
    small_ref[...] = jnp.where(sub < 4, weights, jnp.where(sub == 4, bias, 0.0))

    batch = 16
    total = rows + 8
    diag = lax.broadcasted_iota(jnp.int32, (batch, total, 128), 1) == lax.broadcasted_iota(
        jnp.int32, (batch, total, 128), 2
    )
    for i in range(0, chips, batch):
        part = slice(i, i + batch)
        x = jnp.concatenate([keep_ref[part] + recv_ref[part], small_ref[part]], axis=1)
        largest = jnp.maximum(jnp.max(jnp.abs(x), axis=2, keepdims=True), 1e-30)
        power = jnp.ceil(jnp.log2(largest) * STEPS)
        q = jnp.round(x * (LEVELS * jnp.exp2(power * (-1.0 / STEPS))))
        powers = jnp.sum(jnp.where(diag, power, 0.0), axis=1, keepdims=True)
        tail = jnp.broadcast_to(powers, (batch, 8, 128))
        out_ref[part] = jnp.concatenate([q, tail], axis=1).astype(jnp.int32).astype(jnp.int16)


def last_kernel(z_ref, own_ref, partner_ref, enc_ref, pred_ref, encw_ref, predw_ref, outw_ref, bias_ref):
    core = lax.axis_index("batch")
    first = core == 0
    frame = lax.axis_index("frame")
    rows = z_ref.shape[1] - 8
    big = rows - 8
    n = 8
    width = own_ref.shape[1] // 2
    row = lax.broadcasted_iota(jnp.int32, (rows, 128), 0)
    lane = lax.broadcasted_iota(jnp.int32, (rows, 128), 1)
    diag = row == lane
    total = jnp.zeros((big, 128), F32)
    by_token = [jnp.zeros((8, 128), F32)] * n
    by_frame = [jnp.zeros((8, 128), F32)] * n
    for f in range(n):
        for k in range(n):
            x = z_ref[f * n + k].astype(jnp.int32).astype(F32)
            power = jnp.sum(jnp.where(diag, x[rows : rows + 1], 0.0), axis=1, keepdims=True)
            x = x[:rows] * (jnp.exp2(power * (1.0 / STEPS)) * (1.0 / LEVELS))
            total = total + x[:big]
            by_token[k] = by_token[k] + x[big:]
            by_frame[f] = by_frame[f] + x[big:]
    for v in range(big // 4):
        outw_ref[:, v * 128 : (v + 1) * 128] = total[v * 4 : v * 4 + 4, :]
    bias = jnp.zeros((1, 128), F32)
    for j in range(n):
        cols = slice(j * width, (j + 1) * width)
        encw_ref[:, cols] = by_token[j][:4, :width]
        predw_ref[:, cols] = by_frame[j][:4, width:]
        bias = bias + jnp.where(frame == j, by_token[j][4:5], 0.0)
    offset = lax.axis_index("token") * 8 + core * 4
    bias_ref[...] = pltpu.roll(bias, 128 - offset, 1)[:, :4]
    nt = enc_ref.shape[1]
    own, other = own_ref[:nt, :width], partner_ref[nt:, :width]
    enc_ref[0] = jnp.where(first, own, other)
    pred_ref[0] = jnp.where(first, other, own)


VM = pl.BlockSpec(memory_space=pltpu.VMEM)
HBM = pl.BlockSpec(memory_space=pl.ANY)


def shape(*dims):
    return jax.ShapeDtypeStruct(dims, F32)


def local(
    encoder_out, predictor_out, enc_weight, pred_weight, joint_bias, out_weight,
    blank_occupancy, label_occupancy, frame_lengths, token_lengths, target_ids,
):
    joint, vocab = out_weight.shape
    nf, nt = blank_occupancy.shape[1:]
    width = encoder_out.shape[2]
    core = lax.axis_index("batch")
    n = lax.axis_size("frame")
    groups = [[f * 2 * n + k * 2 for k in range(n)] for f in range(n)]
    groups += [[f * 2 * n + k * 2 + 1 for f in range(n)] for k in range(n)]

    def swap(x):
        return lax.ppermute(x, "batch", [(0, 1), (1, 0)])

    def exchange(x):
        return lax.all_to_all(x, ALL, 0, 0, axis_index_groups=groups)

    enc, pred = encoder_out[0], predictor_out[0]
    keep = jnp.where(core == 0, enc, pred)
    recv = swap(jnp.where(core == 0, pred, enc))
    pair = jnp.concatenate([keep, recv], axis=1)
    gathered = exchange(jnp.broadcast_to(pair[None], (n, nf, 2 * width)))
    partner = swap(gathered)

    cells = nf * nt
    block = FB * nt
    arrays = (gathered, partner, enc_weight, pred_weight, joint_bias[None], blank_occupancy, label_occupancy, target_ids)
    lengths = (frame_lengths, token_lengths)
    term_keep, term_send, stash = pl.pallas_call(
        cells_kernel,
        out_shape=[
            shape(n, nf, 2 * width), shape(n, nf, 2 * width), jax.ShapeDtypeStruct((cells, joint + vocab), BF16),
        ],
        in_specs=[HBM] * 11,
        out_specs=[VM] * 2 + [HBM],
        scratch_shapes=[pltpu.VMEM(x.shape, x.dtype) for x in arrays]
        + [pltpu.SMEM(x.shape, x.dtype) for x in lengths]
        + [
            pltpu.VMEM(out_weight.shape, out_weight.dtype),
            pltpu.SemaphoreType.DMA((11,)),
            pltpu.SemaphoreType.DMA((nf // FB,)),
            pltpu.VMEM((nf, joint), F32),
            pltpu.VMEM((nt, joint), F32),
            pltpu.VMEM((nf, joint), F32),
            pltpu.VMEM((nt, joint), F32),
            pltpu.VMEM((nf, nt), F32),
            pltpu.VMEM((nf, nt), F32),
            pltpu.VMEM((nt, 128), jnp.int32),
            pltpu.VMEM((block, vocab), F32),
            pltpu.VMEM((cells, joint + vocab), BF16),
        ],
        compiler_params=pltpu.CompilerParams(vmem_limit_bytes=BIG),
        name="joint_cells",
    )(*arrays, *lengths, out_weight)

    sums = jnp.concatenate([term_keep, swap(term_send)], axis=1)
    sums, stash = lax.optimization_barrier((sums, stash))
    own = exchange(sums).sum(0)
    rows = vocab // 32
    ow_keep, ow_send, features = pl.pallas_call(
        wgrad_kernel,
        out_shape=[shape(joint // 8, rows, 128)] * 2 + [jax.ShapeDtypeStruct((2, joint, 2 * nt), BF16)],
        in_specs=[HBM] + [VM] * 2,
        out_specs=[VM] * 3,
        scratch_shapes=[
            pltpu.VMEM((cells, joint + vocab), BF16),
            pltpu.VMEM((joint, vocab), F32),
            pltpu.SemaphoreType.DMA((4,)),
        ],
        compiler_params=pltpu.CompilerParams(vmem_limit_bytes=54 * 1024 * 1024),
        cost_estimate=pl.CostEstimate(
            flops=2 * cells * joint * vocab, bytes_accessed=3 * cells * vocab, transcendentals=0
        ),
        name="out_weight_grad",
    )(stash, gathered, partner)
    own, ow_send = lax.optimization_barrier((own, ow_send))
    partner_own = swap(own)
    payload = pl.pallas_call(
        pack_kernel,
        out_shape=jax.ShapeDtypeStruct((joint // 8, rows + 16, 128), jnp.int16),
        in_specs=[VM] * 5,
        out_specs=VM,
        scratch_shapes=[pltpu.VMEM((joint // 8, 8, 2 * width), F32)],
        compiler_params=pltpu.CompilerParams(vmem_limit_bytes=24 * 1024 * 1024),
        name="pack_shares",
    )(ow_keep, swap(ow_send), own, partner_own, features)
    shares = lax.all_to_all(payload, ("frame", "token"), 0, 0)
    own_rows = joint // 128
    enc_grad, pred_grad, enc_wgrad, pred_wgrad, out_wgrad, bias_grad = pl.pallas_call(
        last_kernel,
        out_shape=[
            shape(1, nf, width), shape(1, nt, width), shape(own_rows, joint), shape(own_rows, joint),
            shape(own_rows, vocab), shape(1, own_rows),
        ],
        in_specs=[VM] * 3,
        out_specs=[VM] * 6,
        compiler_params=pltpu.CompilerParams(vmem_limit_bytes=24 * 1024 * 1024),
        name="sum_shares",
    )(shares, own, partner_own)
    return enc_grad, pred_grad, enc_wgrad, pred_wgrad, out_wgrad, bias_grad[0]


def solution(mesh):
    in_specs = (
        P("batch", "frame", "token"),
        P("batch", "token", "frame"),
        P(),
        P(),
        P(),
        P(),
        P("batch", "frame", "token"),
        P("batch", "frame", "token"),
        P(),
        P(),
        P(None, "token"),
    )
    out_specs = (
        P("batch", "frame", "token"),
        P("batch", "token", "frame"),
        P(ALL, None),
        P(ALL, None),
        P(ALL, None),
        P(ALL),
    )
    return jax.shard_map(local, mesh=mesh, in_specs=in_specs, out_specs=out_specs, check_vma=False)
```

```python
import jax
import jax.numpy as jnp
from jax import lax
from jax.experimental import pallas as pl
from jax.experimental.pallas import tpu as pltpu
from jax.sharding import PartitionSpec as P

FB = 16
CHUNK = 256
ALL = ("frame", "token", "batch")
F32, BF16 = jnp.float32, jnp.bfloat16


def split3(x):
    hi = x.astype(BF16)
    rest = x - hi.astype(F32)
    mid = rest.astype(BF16)
    lo = (rest - mid.astype(F32)).astype(BF16)
    return hi, mid, lo


def dot_nt(a, b):
    return lax.dot_general(a, b, (((1,), (1,)), ((), ())), preferred_element_type=F32)


def dot_tn(a, b):
    return lax.dot_general(a, b, (((0,), (0,)), ((), ())), preferred_element_type=F32)


def exact_nt(a, b):
    rows = a.shape[0]
    product = dot_nt(jnp.concatenate(split3(a), axis=0), b)
    return product[:rows] + product[rows : 2 * rows] + product[2 * rows :]


def halves(ref, first_half):
    width = ref.shape[2] // 2
    start = 0 if first_half else width
    pieces = [ref[s].astype(F32)[:, start : start + width] for s in range(ref.shape[0])]
    return jnp.concatenate(pieces, axis=1).astype(BF16)


def exact_tn(a, b):
    return sum(dot_tn(a, piece) for piece in split3(b))


def cells_kernel(
    g_ref, h_ref, weights_ref, cell_ref, keep_ref, send_ref, ow_keep_ref, ow_send_ref, feat_ref,
    encp_ref, predp_ref, rows_ref, prow_ref, tgt_col_ref, occ_ref, e_ref, stash_ref,
):
    nf, nt = encp_ref.shape[0], predp_ref.shape[0]
    joint, vocab = encp_ref.shape[1], e_ref.shape[1]
    encw_ref, predw_ref = weights_ref.at[:joint], weights_ref.at[joint : 2 * joint]
    parts, width = g_ref.shape[0], g_ref.shape[2] // 2
    cells = FB * nt
    first = lax.axis_index("batch") == 0
    own, other = halves(g_ref, True), halves(h_ref, False)
    feat_ref[...] = jnp.concatenate([own.astype(F32).T, halves(g_ref, False).astype(F32).T], axis=1).astype(BF16)
    encp_ref[...] = jnp.dot(jnp.where(first, own, other), encw_ref[...], preferred_element_type=F32)
    predp = jnp.dot(jnp.where(first, other, own), predw_ref[...], preferred_element_type=F32)
    for v in range(joint // 128):
        cols = slice(v * 128, (v + 1) * 128)
        predp_ref[:, cols] = predp[:, cols] + cell_ref[nf + v : nf + v + 1, :]
    diag_row = lax.broadcasted_iota(jnp.int32, (nt, 128), 0)
    diag_lane = lax.broadcasted_iota(jnp.int32, (nt, 128), 1)
    blank_diag, label_diag = diag_row == diag_lane, diag_row + nt == diag_lane
    core = lax.axis_index("batch")
    row = nf + joint // 128
    mine = diag_row + nt * core == diag_lane
    targets = jnp.sum(jnp.where(mine, cell_ref[row : row + 1, :], 0.0), axis=1, keepdims=True)
    tgt_col_ref[...] = jnp.broadcast_to(targets.astype(jnp.int32), (nt, 128))
    lengths = cell_ref[row + 1 : row + 2, :]
    lane1 = diag_lane[:1]
    frame_len = jnp.sum(jnp.where(lane1 == core, lengths, 0.0), axis=1, keepdims=True).astype(jnp.int32)
    token_len = jnp.sum(jnp.where(lane1 == core + 2, lengths, 0.0), axis=1, keepdims=True).astype(jnp.int32)
    frame_pos = lax.axis_index("frame") * nf + lax.broadcasted_iota(jnp.int32, (nf, 128), 0)
    token_pos = lax.axis_index("token") * nt + lax.rem(lax.broadcasted_iota(jnp.int32, (nf, 128), 1), nt)
    reach = jnp.where(lax.broadcasted_iota(jnp.int32, (nf, 128), 1) < nt, token_len, token_len - 1)
    occ_ref[...] = jnp.where((frame_pos < frame_len) & (token_pos <= reach), cell_ref[:nf, :], 0.0)
    prow_ref[...] = jnp.zeros_like(prow_ref)
    lane = lax.broadcasted_iota(jnp.int32, (FB, nt, 128), 2)

    def out_columns(c):
        top, left = divmod(c * CHUNK, joint)
        top = (2 + top) * joint
        return weights_ref[top : top + joint, left : left + CHUNK]

    def columns(diag, t0):
        rows = occ_ref[pl.ds(t0, FB), :]
        return jnp.sum(jnp.where(diag[None], rows[:, None, :], 0.0), axis=2, keepdims=True)

    def block(i, carry):
        t0 = pl.multiple_of(i * FB, FB)
        span = pl.ds(pl.multiple_of(i * cells, cells), cells)
        frames = encp_ref[pl.ds(t0, FB), :]
        inner = frames[:, None, :] + predp_ref[...][None, :, :]
        hidden = jnp.tanh(inner).astype(BF16).reshape(cells, joint)
        stash_ref[span, :joint] = hidden
        total = jnp.zeros((cells, 128), F32)
        for c in range(vocab // CHUNK):
            cols = slice(c * CHUNK, (c + 1) * CHUNK)
            e = jnp.exp(jnp.dot(hidden, out_columns(c), preferred_element_type=F32))
            e_ref[:, cols] = e
            for q in range(CHUNK // 128):
                total = total + e[:, q * 128 : (q + 1) * 128]
        total = jnp.sum(total, axis=1, keepdims=True).reshape(FB, nt, 1)
        bw = columns(blank_diag, t0)
        lw = columns(label_diag, t0)
        scale = (bw + lw) / total
        tgt = tgt_col_ref[...][None]
        for v in range(vocab // 128):
            cols = slice(v * 128, (v + 1) * 128)
            g = e_ref[:, cols].reshape(FB, nt, 128) * scale
            if v == 0:
                g = g - jnp.where(lane == 0, bw, 0.0)
            g = g - jnp.where(lane == tgt - v * 128, lw, 0.0)
            stash_ref[span, joint + v * 128 : joint + (v + 1) * 128] = g.astype(BF16).reshape(cells, 128)
        for c in range(joint // CHUNK):
            cols = slice(c * CHUNK, (c + 1) * CHUNK)
            grad_hidden = sum(
                dot_nt(stash_ref[span, (p + 1) * joint : (p + 2) * joint], weights_ref[(2 + p) * joint + c * CHUNK : (2 + p) * joint + (c + 1) * CHUNK, :])
                for p in range(vocab // joint)
            )
            hf = stash_ref[span, cols].astype(F32)
            gi = (grad_hidden * (1.0 - hf * hf)).reshape(FB, nt, CHUNK)
            prow_ref[:, cols] += gi.sum(0)
            rows_ref[pl.ds(t0, FB), cols] = gi.sum(1)
        return carry

    lax.fori_loop(0, nf // FB, block, 0)

    term_e = exact_nt(rows_ref[...], encw_ref[...])
    term_p = exact_nt(prow_ref[...], predw_ref[...])
    for s in range(parts):
        cols = slice(s * width, (s + 1) * width)
        e_part = jnp.concatenate([term_e[:, cols], rows_ref[:, cols]], axis=1)
        p_part = jnp.concatenate([term_p[:, cols], prow_ref[:, cols]], axis=1)
        keep_ref[s, :nt, :] = jnp.where(first, e_part, p_part)
        send_ref[s] = jnp.where(first, p_part, e_part)

    chips = joint // 8
    top = lax.broadcasted_iota(jnp.int32, (chips, 8, 128), 1) < 4
    half = vocab // 2
    for dest_ref, part in ((ow_send_ref, 1 - core), (ow_keep_ref, core)):
        start = pl.multiple_of(joint + part * half, 128)
        acc = dot_tn(stash_ref[:, :joint], stash_ref[:, pl.ds(start, half)])
        for v in range(half // 256):
            a = acc[:, v * 256 : v * 256 + 128].reshape(chips, 8, 128)
            b = acc[:, v * 256 + 128 : v * 256 + 256].reshape(chips, 8, 128)
            dest_ref[v, :, 0] = jnp.where(top, a, pltpu.roll(b, 4, 1))
            dest_ref[v, :, 1] = jnp.where(top, pltpu.roll(a, 4, 1), b)


LEVELS = 32000.0
STEPS = 16.0
SMALL = 8


def pack_kernel(keep_ref, recv_ref, y_ref, feat_ref, out_ref, total_ref, small_ref):
    tiles, chips = keep_ref.shape[:2]
    big = tiles * 8
    total = y_ref[0]
    for s in range(1, y_ref.shape[0]):
        total = total + y_ref[s]
    total_ref[...] = total
    width = total.shape[1] // 2
    rows_grad = total[:, width:]
    pieces = jnp.concatenate(split3(rows_grad), axis=1)
    product = jnp.dot(feat_ref[...], pieces, preferred_element_type=F32)
    weights = product[:, :width] + product[:, width : 2 * width] + product[:, 2 * width :]
    weights = jnp.concatenate([weights, jnp.zeros_like(weights)], axis=1).reshape(chips, SMALL, 2 * width)
    bias = jnp.sum(rows_grad, axis=0, keepdims=True)
    bias = jnp.concatenate([bias, jnp.zeros_like(bias)], axis=1)[None]
    sub = lax.broadcasted_iota(jnp.int32, weights.shape, 1)
    for c in range(2):
        own = weights if c == 0 else pltpu.roll(weights, 4, 1)
        small_ref[:, c] = jnp.where(sub < 4, own, jnp.where(sub == 4, bias, 0.0))

    batch = 16
    rows = big + SMALL
    row = lax.broadcasted_iota(jnp.int32, (batch, rows, 128), 1)
    diag = row == lax.broadcasted_iota(jnp.int32, (batch, rows, 128), 2)
    for i in range(0, chips, batch // 2):
        part = slice(i, i + batch // 2)
        parts = [keep_ref[v, part] + recv_ref[v, part] for v in range(tiles)] + [small_ref[part]]
        x = jnp.concatenate([p.reshape(batch, 8, 128) for p in parts], axis=1)
        largest = jnp.maximum(jnp.max(jnp.abs(x), axis=2, keepdims=True), 1e-30)
        power = jnp.ceil(jnp.log2(largest) * STEPS)
        q = jnp.round(x * (LEVELS * jnp.exp2(power * (-1.0 / STEPS))))
        powers = jnp.sum(jnp.where(diag, power, 0.0), axis=1, keepdims=True)
        q = jnp.where(row == rows - 1, powers, q)
        out_ref[2 * i : 2 * i + batch] = q.astype(jnp.int32).astype(jnp.int16)


def last_kernel(z_ref, own_ref, partner_ref, enc_ref, pred_ref, encw_ref, predw_ref, outw_ref, bias_ref):
    core = lax.axis_index("batch")
    first = core == 0
    frame = lax.axis_index("frame")
    rows = z_ref.shape[1]
    big = rows - SMALL
    n = 8
    width = own_ref.shape[1] // 2
    row = lax.broadcasted_iota(jnp.int32, (rows, 128), 0)
    lane = lax.broadcasted_iota(jnp.int32, (rows, 128), 1)
    diag = row == lane
    total = [jnp.zeros((big, 128), F32)] * 2
    by_token = [jnp.zeros((SMALL, 128), F32)] * n
    by_frame = [jnp.zeros((SMALL, 128), F32)] * n
    for f in range(n):
        for k in range(n):
            for c in range(2):
                x = z_ref[(f * n + k) * 2 + c].astype(jnp.int32).astype(F32)
                power = jnp.sum(jnp.where(diag, x[rows - 1 :], 0.0), axis=1, keepdims=True)
                x = x * (jnp.exp2(power * (1.0 / STEPS)) * (1.0 / LEVELS))
                total[c] = total[c] + x[:big]
                if c == 0:
                    by_token[k] = by_token[k] + x[big:]
                else:
                    by_frame[f] = by_frame[f] + x[big:]
    for c in range(2):
        for t in range(big // 4):
            v = c * (big // 4) + t
            outw_ref[:, v * 128 : (v + 1) * 128] = total[c][t * 4 : t * 4 + 4, :]
    bias = jnp.zeros((1, 128), F32)
    for j in range(n):
        cols = slice(j * width, (j + 1) * width)
        encw_ref[:, cols] = by_token[j][:4, :width]
        predw_ref[:, cols] = by_frame[j][:4, :width]
        bias = bias + jnp.where(frame == j, by_token[j][4:5], 0.0)
    offset = lax.axis_index("token") * 8 + core * 4
    bias_ref[...] = pltpu.roll(bias, 128 - offset, 1)[:, :4]
    nt = enc_ref.shape[1]
    own, other = own_ref[:nt, :width], partner_ref[nt:, :width]
    enc_ref[0] = jnp.where(first, own, other)
    pred_ref[0] = jnp.where(first, other, own)


VM = pl.BlockSpec(memory_space=pltpu.VMEM)


def shape(*dims):
    return jax.ShapeDtypeStruct(dims, F32)


def local(
    encoder_out, predictor_out, enc_weight, pred_weight, joint_bias, out_weight,
    blank_occupancy, label_occupancy, frame_lengths, token_lengths, target_ids,
):
    joint, vocab = out_weight.shape
    nf, nt = blank_occupancy.shape[1:]
    width = encoder_out.shape[2]
    core = lax.axis_index("batch")
    n = lax.axis_size("frame")
    groups = [[f * 2 * n + k * 2 for k in range(n)] for f in range(n)]
    groups += [[f * 2 * n + k * 2 + 1 for f in range(n)] for k in range(n)]

    def swap(x):
        return lax.ppermute(x, "batch", [(0, 1), (1, 0)])

    def exchange(x):
        return lax.all_to_all(x, ALL, 0, 0, axis_index_groups=groups)

    enc, pred = encoder_out[0], predictor_out[0]
    keep = jnp.where(core == 0, enc, pred)
    recv = swap(jnp.where(core == 0, pred, enc))
    pair = jnp.concatenate([keep, recv], axis=1)
    payload = jnp.broadcast_to(pair[None], (n, nf, 2 * width))
    lengths = jnp.concatenate([frame_lengths, token_lengths])
    payload, enc_weight, pred_weight, out_weight, blank_occupancy, label_occupancy, joint_bias, target_ids, lengths = (
        lax.optimization_barrier((
            payload, enc_weight, pred_weight, out_weight, blank_occupancy, label_occupancy, joint_bias, target_ids,
            lengths,
        ))
    )
    gathered = exchange(payload)

    cells = nf * nt
    per_cell = jnp.concatenate(
        [
            jnp.concatenate([blank_occupancy[0], label_occupancy[0]], axis=1),
            joint_bias.reshape(joint // 128, 128),
            target_ids.astype(F32).reshape(1, 2 * nt),
            jnp.pad(lengths.astype(F32)[None], ((0, 2), (0, 128 - lengths.shape[0]))),
        ],
        axis=0,
    )
    halves_of_out = [out_weight[:, i : i + joint] for i in range(0, vocab, joint)]
    weights = jnp.concatenate([enc_weight, pred_weight, *halves_of_out], axis=0)
    gathered, weights, per_cell = lax.optimization_barrier((gathered, weights, per_cell))
    partner = swap(gathered)
    tiles = vocab // 512
    term_keep, term_send, ow_keep, ow_send, features = pl.pallas_call(
        cells_kernel,
        out_shape=[shape(n, 2 * nf, 2 * width), shape(n, nf, 2 * width)]
        + [shape(tiles, joint // 8, 2, 8, 128)] * 2
        + [jax.ShapeDtypeStruct((joint, 2 * nt), BF16)],
        in_specs=[VM] * 4,
        out_specs=[VM] * 5,
        scratch_shapes=[
            pltpu.VMEM((nf, joint), F32),
            pltpu.VMEM((nt, joint), F32),
            pltpu.VMEM((nf, joint), F32),
            pltpu.VMEM((nt, joint), F32),
            pltpu.VMEM((nt, 128), jnp.int32),
            pltpu.VMEM((nf, 2 * nt), F32),
            pltpu.VMEM((FB * nt, vocab), F32),
            pltpu.VMEM((cells, joint + vocab), BF16),
        ],
        compiler_params=pltpu.CompilerParams(vmem_limit_bytes=40 * 1024 * 1024),
        name="joint_cells",
    )(gathered, partner, weights, per_cell)

    sums = lax.dynamic_update_slice(term_keep, swap(term_send), (0, nf, 0))
    summed = exchange(sums)
    payload, own = pl.pallas_call(
        pack_kernel,
        out_shape=[
            jax.ShapeDtypeStruct((joint // 4, tiles * 8 + SMALL, 128), jnp.int16),
            shape(2 * nf, 2 * width),
        ],
        in_specs=[VM] * 4,
        out_specs=[VM] * 2,
        scratch_shapes=[pltpu.VMEM((joint // 8, 2, SMALL, 2 * width), F32)],
        compiler_params=pltpu.CompilerParams(vmem_limit_bytes=16 * 1024 * 1024),
        name="pack_shares",
    )(ow_keep, swap(ow_send), summed, features)
    partner_own = swap(own)
    shares = lax.all_to_all(payload, ALL, 0, 0)
    own_rows = joint // 128
    enc_grad, pred_grad, enc_wgrad, pred_wgrad, out_wgrad, bias_grad = pl.pallas_call(
        last_kernel,
        out_shape=[
            shape(1, nf, width), shape(1, nt, width), shape(own_rows, joint), shape(own_rows, joint),
            shape(own_rows, vocab), shape(1, own_rows),
        ],
        in_specs=[VM] * 3,
        out_specs=[VM] * 6,
        compiler_params=pltpu.CompilerParams(vmem_limit_bytes=24 * 1024 * 1024),
        name="sum_shares",
    )(shares, own, partner_own)
    return enc_grad, pred_grad, enc_wgrad, pred_wgrad, out_wgrad, bias_grad[0]


def solution(mesh):
    in_specs = (
        P("batch", "frame", "token"),
        P("batch", "token", "frame"),
        P(),
        P(),
        P(),
        P(),
        P("batch", "frame", "token"),
        P("batch", "frame", "token"),
        P(),
        P(),
        P(None, "token"),
    )
    out_specs = (
        P("batch", "frame", "token"),
        P("batch", "token", "frame"),
        P(ALL, None),
        P(ALL, None),
        P(ALL, None),
        P(ALL),
    )
    return jax.shard_map(local, mesh=mesh, in_specs=in_specs, out_specs=out_specs, check_vma=False)
```

```python
import jax
import jax.numpy as jnp
from jax import lax
from jax.experimental import pallas as pl
from jax.experimental.pallas import tpu as pltpu
from jax.sharding import PartitionSpec as P

FB = 16
CHUNK = 256
LEVELS = 32000.0
STEPS = 16.0
SMALL = 8
TAIL = 16
ALL = ("frame", "token", "batch")
F32, BF16 = jnp.float32, jnp.bfloat16


def split3(x):
    hi = x.astype(BF16)
    rest = x - hi.astype(F32)
    mid = rest.astype(BF16)
    lo = (rest - mid.astype(F32)).astype(BF16)
    return hi, mid, lo


def dot_nt(a, b):
    return lax.dot_general(a, b, (((1,), (1,)), ((), ())), preferred_element_type=F32)


def dot_tn(a, b):
    return lax.dot_general(a, b, (((0,), (0,)), ((), ())), preferred_element_type=F32)


def exact_nt(a, b):
    rows = a.shape[0]
    product = dot_nt(jnp.concatenate(split3(a), axis=0), b)
    return product[:rows] + product[rows : 2 * rows] + product[2 * rows :]


def to_levels(x):
    largest = jnp.maximum(jnp.max(jnp.abs(x), axis=-1, keepdims=True), 1e-30)
    power = jnp.ceil(jnp.log2(largest) * STEPS)
    return jnp.round(x * (LEVELS * jnp.exp2(power * (-1.0 / STEPS)))), power


def from_levels(x, powers):
    rows = x.shape[0]
    diag = lax.broadcasted_iota(jnp.int32, (rows, 128), 0) == lax.broadcasted_iota(jnp.int32, (rows, 128), 1)
    power = jnp.sum(jnp.where(diag, powers, 0.0), axis=1, keepdims=True)
    return x * (jnp.exp2(power * (1.0 / STEPS)) * (1.0 / LEVELS))


def halves(ref, first_half):
    width = ref.shape[2] // 2
    start = 0 if first_half else width
    pieces = [ref[s].astype(F32)[:, start : start + width] for s in range(ref.shape[0])]
    return jnp.concatenate(pieces, axis=1).astype(BF16)


def exact_tn(a, b):
    return sum(dot_tn(a, piece) for piece in split3(b))


def cells_kernel(
    g_ref, h_ref, weights_ref, cell_ref, keep_ref, send_ref, ow_keep_ref, ow_send_ref, feat_ref,
    encp_ref, predp_ref, rows_ref, prow_ref, tgt_col_ref, occ_ref, e_ref, stash_ref,
):
    nf, nt = encp_ref.shape[0], predp_ref.shape[0]
    joint, vocab = encp_ref.shape[1], e_ref.shape[1]
    ow_ref = weights_ref.at[:, :vocab]
    encw_ref = weights_ref.at[:, vocab : vocab + joint]
    predw_ref = weights_ref.at[:, vocab + joint :]
    parts, width = g_ref.shape[0], g_ref.shape[2] // 2
    cells = FB * nt
    first = lax.axis_index("batch") == 0
    own, other = halves(g_ref, True), halves(h_ref, False)
    feat_ref[...] = jnp.concatenate([own.astype(F32).T, halves(g_ref, False).astype(F32).T], axis=1).astype(BF16)
    encp_ref[...] = jnp.dot(jnp.where(first, own, other), encw_ref[...], preferred_element_type=F32)
    predp = jnp.dot(jnp.where(first, other, own), predw_ref[...], preferred_element_type=F32)
    for v in range(joint // 128):
        cols = slice(v * 128, (v + 1) * 128)
        predp_ref[:, cols] = predp[:, cols] + cell_ref[nf + v : nf + v + 1, :]
    diag_row = lax.broadcasted_iota(jnp.int32, (nt, 128), 0)
    diag_lane = lax.broadcasted_iota(jnp.int32, (nt, 128), 1)
    blank_diag, label_diag = diag_row == diag_lane, diag_row + nt == diag_lane
    core = lax.axis_index("batch")
    row = nf + joint // 128
    mine = diag_row + nt * core == diag_lane
    targets = jnp.sum(jnp.where(mine, cell_ref[row : row + 1, :], 0.0), axis=1, keepdims=True)
    tgt_col_ref[...] = jnp.broadcast_to(targets.astype(jnp.int32), (nt, 128))
    lengths = cell_ref[row + 1 : row + 2, :]
    lane1 = diag_lane[:1]
    frame_len = jnp.sum(jnp.where(lane1 == core, lengths, 0.0), axis=1, keepdims=True).astype(jnp.int32)
    token_len = jnp.sum(jnp.where(lane1 == core + 2, lengths, 0.0), axis=1, keepdims=True).astype(jnp.int32)
    frame_pos = lax.axis_index("frame") * nf + lax.broadcasted_iota(jnp.int32, (nf, 128), 0)
    token_pos = lax.axis_index("token") * nt + lax.rem(lax.broadcasted_iota(jnp.int32, (nf, 128), 1), nt)
    reach = jnp.where(lax.broadcasted_iota(jnp.int32, (nf, 128), 1) < nt, token_len, token_len - 1)
    occ_ref[...] = jnp.where((frame_pos < frame_len) & (token_pos <= reach), cell_ref[:nf, :], 0.0)
    prow_ref[...] = jnp.zeros_like(prow_ref)
    lane = lax.broadcasted_iota(jnp.int32, (FB, nt, 128), 2)

    def columns(diag, t0):
        rows = occ_ref[pl.ds(t0, FB), :]
        return jnp.sum(jnp.where(diag[None], rows[:, None, :], 0.0), axis=2, keepdims=True)

    def block(i, carry):
        t0 = pl.multiple_of(i * FB, FB)
        span = pl.ds(pl.multiple_of(i * cells, cells), cells)
        frames = encp_ref[pl.ds(t0, FB), :]
        inner = frames[:, None, :] + predp_ref[...][None, :, :]
        hidden = jnp.tanh(inner).astype(BF16).reshape(cells, joint)
        stash_ref[span, :joint] = hidden
        total = jnp.zeros((cells, 128), F32)
        for c in range(vocab // CHUNK):
            cols = slice(c * CHUNK, (c + 1) * CHUNK)
            e = jnp.exp(jnp.dot(hidden, ow_ref[:, cols], preferred_element_type=F32))
            e_ref[:, cols] = e
            for q in range(CHUNK // 128):
                total = total + e[:, q * 128 : (q + 1) * 128]
        total = jnp.sum(total, axis=1, keepdims=True).reshape(FB, nt, 1)
        bw = columns(blank_diag, t0)
        lw = columns(label_diag, t0)
        scale = (bw + lw) / total
        tgt = tgt_col_ref[...][None]
        for v in range(vocab // 128):
            cols = slice(v * 128, (v + 1) * 128)
            g = e_ref[:, cols].reshape(FB, nt, 128) * scale
            if v == 0:
                g = g - jnp.where(lane == 0, bw, 0.0)
            g = g - jnp.where(lane == tgt - v * 128, lw, 0.0)
            stash_ref[span, joint + v * 128 : joint + (v + 1) * 128] = g.astype(BF16).reshape(cells, 128)
        for c in range(joint // CHUNK):
            cols = slice(c * CHUNK, (c + 1) * CHUNK)
            grad_hidden = dot_nt(stash_ref[span, joint:], ow_ref[cols, :])
            hf = stash_ref[span, cols].astype(F32)
            gi = (grad_hidden * (1.0 - hf * hf)).reshape(FB, nt, CHUNK)
            prow_ref[:, cols] += gi.sum(0)
            rows_ref[pl.ds(t0, FB), cols] = gi.sum(1)
        return carry

    lax.fori_loop(0, nf // FB, block, 0)

    term_e = exact_nt(rows_ref[...], encw_ref[...])
    term_p = exact_nt(prow_ref[...], predw_ref[...])
    for s in range(parts):
        cols = slice(s * width, (s + 1) * width)
        e_part = jnp.concatenate([term_e[:, cols], rows_ref[:, cols]], axis=1)
        p_part = jnp.concatenate([term_p[:, cols], prow_ref[:, cols]], axis=1)
        for ref, part in ((keep_ref, jnp.where(first, e_part, p_part)), (send_ref, jnp.where(first, p_part, e_part))):
            q, power = to_levels(part)
            powers = jnp.sum(jnp.where(blank_diag, power, 0.0), axis=0, keepdims=True)
            q = jnp.concatenate([q, jnp.broadcast_to(powers, (TAIL, 128))], axis=0)
            ref[s, : nt + TAIL, :] = q.astype(jnp.int32).astype(jnp.int16)

    chips = joint // 8
    top = lax.broadcasted_iota(jnp.int32, (chips, 8, 128), 1) < 4
    half = vocab // 2
    for dest_ref, part in ((ow_send_ref, 1 - core), (ow_keep_ref, core)):
        start = pl.multiple_of(joint + part * half, 128)
        acc = dot_tn(stash_ref[:, :joint], stash_ref[:, pl.ds(start, half)])
        for v in range(half // 256):
            a = acc[:, v * 256 : v * 256 + 128].reshape(chips, 8, 128)
            b = acc[:, v * 256 + 128 : v * 256 + 256].reshape(chips, 8, 128)
            dest_ref[v, :, 0] = jnp.where(top, a, pltpu.roll(b, 4, 1))
            dest_ref[v, :, 1] = jnp.where(top, pltpu.roll(a, 4, 1), b)


def pack_kernel(keep_ref, recv_ref, y_ref, feat_ref, out_ref, total_ref, small_ref):
    tiles, chips = keep_ref.shape[:2]
    big = tiles * 8
    span = y_ref.shape[1] // 2
    nt = span - TAIL
    for h in range(2):
        total = jnp.zeros((nt, y_ref.shape[2]), F32)
        for s in range(y_ref.shape[0]):
            x = y_ref[s, h * span : (h + 1) * span, :].astype(jnp.int32).astype(F32)
            total = total + from_levels(x[:nt], x[nt : nt + 1])
        total_ref[h * nt : (h + 1) * nt, :] = total
    total = total_ref[...]
    width = total.shape[1] // 2
    rows_grad = total[:, width:]
    pieces = jnp.concatenate(split3(rows_grad), axis=1)
    product = jnp.dot(feat_ref[...], pieces, preferred_element_type=F32)
    weights = product[:, :width] + product[:, width : 2 * width] + product[:, 2 * width :]
    weights = jnp.concatenate([weights, jnp.zeros_like(weights)], axis=1).reshape(chips, SMALL, 2 * width)
    bias = jnp.sum(rows_grad, axis=0, keepdims=True)
    bias = jnp.concatenate([bias, jnp.zeros_like(bias)], axis=1)[None]
    sub = lax.broadcasted_iota(jnp.int32, weights.shape, 1)
    for c in range(2):
        own = weights if c == 0 else pltpu.roll(weights, 4, 1)
        small_ref[:, c] = jnp.where(sub < 4, own, jnp.where(sub == 4, bias, 0.0))

    batch = 16
    rows = big + SMALL
    row = lax.broadcasted_iota(jnp.int32, (batch, rows, 128), 1)
    diag = row == lax.broadcasted_iota(jnp.int32, (batch, rows, 128), 2)
    for i in range(0, chips, batch // 2):
        part = slice(i, i + batch // 2)
        parts = [keep_ref[v, part] + recv_ref[v, part] for v in range(tiles)] + [small_ref[part]]
        x = jnp.concatenate([p.reshape(batch, 8, 128) for p in parts], axis=1)
        q, power = to_levels(x)
        powers = jnp.sum(jnp.where(diag, power, 0.0), axis=1, keepdims=True)
        q = jnp.where(row == rows - 1, powers, q)
        out_ref[2 * i : 2 * i + batch] = q.astype(jnp.int32).astype(jnp.int16)


def last_kernel(z_ref, own_ref, partner_ref, enc_ref, pred_ref, encw_ref, predw_ref, outw_ref, bias_ref):
    core = lax.axis_index("batch")
    first = core == 0
    frame = lax.axis_index("frame")
    rows = z_ref.shape[1]
    big = rows - SMALL
    n = 8
    width = own_ref.shape[1] // 2
    total = [jnp.zeros((big, 128), F32)] * 2
    by_token = [jnp.zeros((SMALL, 128), F32)] * n
    by_frame = [jnp.zeros((SMALL, 128), F32)] * n
    for f in range(n):
        for k in range(n):
            for c in range(2):
                x = z_ref[(f * n + k) * 2 + c].astype(jnp.int32).astype(F32)
                x = from_levels(x, x[rows - 1 :])
                total[c] = total[c] + x[:big]
                if c == 0:
                    by_token[k] = by_token[k] + x[big:]
                else:
                    by_frame[f] = by_frame[f] + x[big:]
    for c in range(2):
        for t in range(big // 4):
            v = c * (big // 4) + t
            outw_ref[:, v * 128 : (v + 1) * 128] = total[c][t * 4 : t * 4 + 4, :]
    bias = jnp.zeros((1, 128), F32)
    for j in range(n):
        cols = slice(j * width, (j + 1) * width)
        encw_ref[:, cols] = by_token[j][:4, :width]
        predw_ref[:, cols] = by_frame[j][:4, :width]
        bias = bias + jnp.where(frame == j, by_token[j][4:5], 0.0)
    offset = lax.axis_index("token") * 8 + core * 4
    bias_ref[...] = pltpu.roll(bias, 128 - offset, 1)[:, :4]
    nt = enc_ref.shape[1]
    own, other = own_ref[:nt, :width], partner_ref[nt:, :width]
    enc_ref[0] = jnp.where(first, own, other)
    pred_ref[0] = jnp.where(first, other, own)


VM = pl.BlockSpec(memory_space=pltpu.VMEM)


def shape(*dims):
    return jax.ShapeDtypeStruct(dims, F32)


def local(
    encoder_out, predictor_out, enc_weight, pred_weight, joint_bias, out_weight,
    blank_occupancy, label_occupancy, frame_lengths, token_lengths, target_ids,
):
    joint, vocab = out_weight.shape
    nf, nt = blank_occupancy.shape[1:]
    width = encoder_out.shape[2]
    core = lax.axis_index("batch")
    n = lax.axis_size("frame")
    groups = [[f * 2 * n + k * 2 for k in range(n)] for f in range(n)]
    groups += [[f * 2 * n + k * 2 + 1 for f in range(n)] for k in range(n)]

    def swap(x):
        return lax.ppermute(x, "batch", [(0, 1), (1, 0)])

    def exchange(x):
        return lax.all_to_all(x, ALL, 0, 0, axis_index_groups=groups)

    enc, pred = encoder_out[0], predictor_out[0]
    def spread(own, other):
        return jnp.broadcast_to(jnp.where(core == 0, own, other)[None], (n, nf, width))

    payload = jnp.concatenate([spread(enc, pred), spread(swap(enc), swap(pred))], axis=2)
    (
        payload, enc_weight, pred_weight, out_weight, blank_occupancy, label_occupancy, joint_bias, target_ids,
        frame_lengths, token_lengths,
    ) = lax.optimization_barrier((
        payload, enc_weight, pred_weight, out_weight, blank_occupancy, label_occupancy, joint_bias, target_ids,
        frame_lengths, token_lengths,
    ))
    gathered = exchange(payload)

    cells = nf * nt
    lengths = jnp.concatenate([frame_lengths, token_lengths])
    per_cell = jnp.concatenate(
        [
            jnp.concatenate([blank_occupancy[0], label_occupancy[0]], axis=1),
            joint_bias.reshape(joint // 128, 128),
            target_ids.astype(F32).reshape(1, 2 * nt),
            jnp.pad(lengths.astype(F32)[None], ((0, 2), (0, 128 - lengths.shape[0]))),
        ],
        axis=0,
    )
    weights = jnp.concatenate([out_weight, enc_weight, pred_weight], axis=1)
    gathered, weights, per_cell = lax.optimization_barrier((gathered, weights, per_cell))
    partner = swap(gathered)
    tiles = vocab // 512
    term_keep, term_send, ow_keep, ow_send, features = pl.pallas_call(
        cells_kernel,
        out_shape=[
            jax.ShapeDtypeStruct((n, 2 * (nf + TAIL), 2 * width), jnp.int16),
            jax.ShapeDtypeStruct((n, nf + TAIL, 2 * width), jnp.int16),
        ]
        + [shape(tiles, joint // 8, 2, 8, 128)] * 2
        + [jax.ShapeDtypeStruct((joint, 2 * nt), BF16)],
        in_specs=[VM] * 4,
        out_specs=[VM] * 5,
        scratch_shapes=[
            pltpu.VMEM((nf, joint), F32),
            pltpu.VMEM((nt, joint), F32),
            pltpu.VMEM((nf, joint), F32),
            pltpu.VMEM((nt, joint), F32),
            pltpu.VMEM((nt, 128), jnp.int32),
            pltpu.VMEM((nf, 2 * nt), F32),
            pltpu.VMEM((FB * nt, vocab), F32),
            pltpu.VMEM((cells, joint + vocab), BF16),
        ],
        compiler_params=pltpu.CompilerParams(vmem_limit_bytes=40 * 1024 * 1024),
        name="joint_cells",
    )(gathered, partner, weights, per_cell)

    term_recv, ow_send = lax.optimization_barrier((swap(term_send), ow_send))
    ow_recv = swap(ow_send)
    sums = lax.dynamic_update_slice(term_keep, term_recv, (0, nf + TAIL, 0))
    summed = exchange(sums)
    payload, own = pl.pallas_call(
        pack_kernel,
        out_shape=[
            jax.ShapeDtypeStruct((joint // 4, tiles * 8 + SMALL, 128), jnp.int16),
            shape(2 * nf, 2 * width),
        ],
        in_specs=[VM] * 4,
        out_specs=[VM] * 2,
        scratch_shapes=[pltpu.VMEM((joint // 8, 2, SMALL, 2 * width), F32)],
        compiler_params=pltpu.CompilerParams(vmem_limit_bytes=16 * 1024 * 1024),
        name="pack_shares",
    )(ow_keep, ow_recv, summed, features)
    partner_own = swap(own)
    shares = lax.all_to_all(payload, ALL, 0, 0)
    own_rows = joint // 128
    enc_grad, pred_grad, enc_wgrad, pred_wgrad, out_wgrad, bias_grad = pl.pallas_call(
        last_kernel,
        out_shape=[
            shape(1, nf, width), shape(1, nt, width), shape(own_rows, joint), shape(own_rows, joint),
            shape(own_rows, vocab), shape(1, own_rows),
        ],
        in_specs=[VM] * 3,
        out_specs=[VM] * 6,
        compiler_params=pltpu.CompilerParams(vmem_limit_bytes=24 * 1024 * 1024),
        name="sum_shares",
    )(shares, own, partner_own)
    return enc_grad, pred_grad, enc_wgrad, pred_wgrad, out_wgrad, bias_grad[0]


def solution(mesh):
    in_specs = (
        P("batch", "frame", "token"),
        P("batch", "token", "frame"),
        P(),
        P(),
        P(),
        P(),
        P("batch", "frame", "token"),
        P("batch", "frame", "token"),
        P(),
        P(),
        P(None, "token"),
    )
    out_specs = (
        P("batch", "frame", "token"),
        P("batch", "token", "frame"),
        P(ALL, None),
        P(ALL, None),
        P(ALL, None),
        P(ALL),
    )
    return jax.shard_map(local, mesh=mesh, in_specs=in_specs, out_specs=out_specs, check_vma=False)
```

```python
import jax
import jax.numpy as jnp
from jax import lax
from jax.experimental import pallas as pl
from jax.experimental.pallas import tpu as pltpu
from jax.sharding import PartitionSpec as P

FB = 16
CHUNK = 256
LEVELS = 32000.0
STEPS = 16.0
SMALL = 8
TAIL = 16
ALL = ("frame", "token", "batch")
F32, BF16 = jnp.float32, jnp.bfloat16


def split3(x):
    hi = x.astype(BF16)
    rest = x - hi.astype(F32)
    mid = rest.astype(BF16)
    lo = (rest - mid.astype(F32)).astype(BF16)
    return hi, mid, lo


def dot_nt(a, b):
    return lax.dot_general(a, b, (((1,), (1,)), ((), ())), preferred_element_type=F32)


def dot_tn(a, b):
    return lax.dot_general(a, b, (((0,), (0,)), ((), ())), preferred_element_type=F32)


def exact_nt(a, b):
    rows = a.shape[0]
    product = dot_nt(jnp.concatenate(split3(a), axis=0), b)
    return product[:rows] + product[rows : 2 * rows] + product[2 * rows :]


def to_levels(x):
    largest = jnp.maximum(jnp.max(jnp.abs(x), axis=-1, keepdims=True), 1e-30)
    power = jnp.ceil(jnp.log2(largest) * STEPS)
    return jnp.round(x * (LEVELS * jnp.exp2(power * (-1.0 / STEPS)))), power


def from_levels(x, powers):
    rows = x.shape[0]
    diag = lax.broadcasted_iota(jnp.int32, (rows, 128), 0) == lax.broadcasted_iota(jnp.int32, (rows, 128), 1)
    power = jnp.sum(jnp.where(diag, powers, 0.0), axis=1, keepdims=True)
    return x * (jnp.exp2(power * (1.0 / STEPS)) * (1.0 / LEVELS))


def halves(ref, first_half):
    width = ref.shape[2] // 2
    start = 0 if first_half else width
    pieces = [ref[s].astype(F32)[:, start : start + width] for s in range(ref.shape[0])]
    return jnp.concatenate(pieces, axis=1).astype(BF16)


def exact_tn(a, b):
    return sum(dot_tn(a, piece) for piece in split3(b))


def cells_kernel(
    g_ref, h_ref, weights_ref, cell_ref, keep_ref, send_ref, ow_keep_ref, ow_send_ref, feat_ref,
    encp_ref, predp_ref, rows_ref, prow_ref, tgt_col_ref, occ_ref, e_ref, stash_ref,
):
    nf, nt = encp_ref.shape[0], predp_ref.shape[0]
    joint, vocab = encp_ref.shape[1], e_ref.shape[1]
    ow_ref = weights_ref.at[:, :vocab]
    encw_ref = weights_ref.at[:, vocab : vocab + joint]
    predw_ref = weights_ref.at[:, vocab + joint :]
    parts, width = g_ref.shape[0], g_ref.shape[2] // 2
    cells = FB * nt
    first = lax.axis_index("batch") == 0
    own, other = halves(g_ref, True), halves(h_ref, False)
    feat_ref[...] = jnp.concatenate([own.astype(F32).T, halves(g_ref, False).astype(F32).T], axis=1).astype(BF16)
    encp_ref[...] = jnp.dot(jnp.where(first, own, other), encw_ref[...], preferred_element_type=F32)
    predp = jnp.dot(jnp.where(first, other, own), predw_ref[...], preferred_element_type=F32)
    for v in range(joint // 128):
        cols = slice(v * 128, (v + 1) * 128)
        predp_ref[:, cols] = predp[:, cols] + cell_ref[nf + v : nf + v + 1, :]
    diag_row = lax.broadcasted_iota(jnp.int32, (nt, 128), 0)
    diag_lane = lax.broadcasted_iota(jnp.int32, (nt, 128), 1)
    blank_diag, label_diag = diag_row == diag_lane, diag_row + nt == diag_lane
    core = lax.axis_index("batch")
    row = nf + joint // 128
    mine = diag_row + nt * core == diag_lane
    targets = jnp.sum(jnp.where(mine, cell_ref[row : row + 1, :], 0.0), axis=1, keepdims=True)
    tgt_col_ref[...] = jnp.broadcast_to(targets.astype(jnp.int32), (nt, 128))
    lengths = cell_ref[row + 1 : row + 2, :]
    lane1 = diag_lane[:1]
    frame_len = jnp.sum(jnp.where(lane1 == core, lengths, 0.0), axis=1, keepdims=True).astype(jnp.int32)
    token_len = jnp.sum(jnp.where(lane1 == core + 2, lengths, 0.0), axis=1, keepdims=True).astype(jnp.int32)
    frame_pos = lax.axis_index("frame") * nf + lax.broadcasted_iota(jnp.int32, (nf, 128), 0)
    token_pos = lax.axis_index("token") * nt + lax.rem(lax.broadcasted_iota(jnp.int32, (nf, 128), 1), nt)
    reach = jnp.where(lax.broadcasted_iota(jnp.int32, (nf, 128), 1) < nt, token_len, token_len - 1)
    occ_ref[...] = jnp.where((frame_pos < frame_len) & (token_pos <= reach), cell_ref[:nf, :], 0.0)
    prow_ref[...] = jnp.zeros_like(prow_ref)
    lane = lax.broadcasted_iota(jnp.int32, (FB, nt, 128), 2)

    def columns(diag, t0):
        rows = occ_ref[pl.ds(t0, FB), :]
        return jnp.sum(jnp.where(diag[None], rows[:, None, :], 0.0), axis=2, keepdims=True)

    def block(i, carry):
        t0 = pl.multiple_of(i * FB, FB)
        span = pl.ds(pl.multiple_of(i * cells, cells), cells)
        frames = encp_ref[pl.ds(t0, FB), :]
        inner = frames[:, None, :] + predp_ref[...][None, :, :]
        hidden = jnp.tanh(inner).astype(BF16).reshape(cells, joint)
        stash_ref[span, :joint] = hidden
        total = jnp.zeros((cells, 128), F32)
        for c in range(vocab // CHUNK):
            cols = slice(c * CHUNK, (c + 1) * CHUNK)
            e = jnp.exp(jnp.dot(hidden, ow_ref[:, cols], preferred_element_type=F32))
            e_ref[:, cols] = e
            for q in range(CHUNK // 128):
                total = total + e[:, q * 128 : (q + 1) * 128]
        total = jnp.sum(total, axis=1, keepdims=True).reshape(FB, nt, 1)
        bw = columns(blank_diag, t0)
        lw = columns(label_diag, t0)
        scale = (bw + lw) / total
        tgt = tgt_col_ref[...][None]
        for v in range(vocab // 128):
            cols = slice(v * 128, (v + 1) * 128)
            g = e_ref[:, cols].reshape(FB, nt, 128) * scale
            if v == 0:
                g = g - jnp.where(lane == 0, bw, 0.0)
            g = g - jnp.where(lane == tgt - v * 128, lw, 0.0)
            stash_ref[span, joint + v * 128 : joint + (v + 1) * 128] = g.astype(BF16).reshape(cells, 128)
        for c in range(joint // CHUNK):
            cols = slice(c * CHUNK, (c + 1) * CHUNK)
            grad_hidden = dot_nt(stash_ref[span, joint:], ow_ref[cols, :])
            hf = stash_ref[span, cols].astype(F32)
            gi = (grad_hidden * (1.0 - hf * hf)).reshape(FB, nt, CHUNK)
            prow_ref[:, cols] += gi.sum(0)
            rows_ref[pl.ds(t0, FB), cols] = gi.sum(1)
        return carry

    lax.fori_loop(0, nf // FB, block, 0)

    term_e = exact_nt(rows_ref[...], encw_ref[...])
    term_p = exact_nt(prow_ref[...], predw_ref[...])
    for s in range(parts):
        cols = slice(s * width, (s + 1) * width)
        e_part = jnp.concatenate([term_e[:, cols], rows_ref[:, cols]], axis=1)
        p_part = jnp.concatenate([term_p[:, cols], prow_ref[:, cols]], axis=1)
        for ref, part in ((keep_ref, jnp.where(first, e_part, p_part)), (send_ref, jnp.where(first, p_part, e_part))):
            q, power = to_levels(part)
            powers = jnp.sum(jnp.where(blank_diag, power, 0.0), axis=0, keepdims=True)
            q = jnp.concatenate([q, jnp.broadcast_to(powers, (TAIL, 128))], axis=0)
            ref[s, : nt + TAIL, :] = q.astype(jnp.int32).astype(jnp.int16)

    chips = joint // 8
    top = lax.broadcasted_iota(jnp.int32, (chips, 8, 128), 1) < 4
    half = vocab // 2
    for dest_ref, part in ((ow_send_ref, 1 - core), (ow_keep_ref, core)):
        start = pl.multiple_of(joint + part * half, 128)
        acc = dot_tn(stash_ref[:, :joint], stash_ref[:, pl.ds(start, half)])
        for v in range(half // 256):
            a = acc[:, v * 256 : v * 256 + 128].reshape(chips, 8, 128)
            b = acc[:, v * 256 + 128 : v * 256 + 256].reshape(chips, 8, 128)
            dest_ref[v, :, 0] = jnp.where(top, a, pltpu.roll(b, 4, 1))
            dest_ref[v, :, 1] = jnp.where(top, pltpu.roll(a, 4, 1), b)


def sum_kernel(y_ref, total_ref):
    span = y_ref.shape[1] // 2
    nt = span - TAIL
    for h in range(2):
        total = jnp.zeros((nt, y_ref.shape[2]), F32)
        for s in range(y_ref.shape[0]):
            x = y_ref[s, h * span : (h + 1) * span, :].astype(jnp.int32).astype(F32)
            total = total + from_levels(x[:nt], x[nt : nt + 1])
        total_ref[h * nt : (h + 1) * nt, :] = total


def pack_kernel(keep_ref, recv_ref, total_ref, feat_ref, out_ref, small_ref):
    tiles, chips = keep_ref.shape[:2]
    big = tiles * 8
    total = total_ref[...]
    width = total.shape[1] // 2
    rows_grad = total[:, width:]
    pieces = jnp.concatenate(split3(rows_grad), axis=1)
    product = jnp.dot(feat_ref[...], pieces, preferred_element_type=F32)
    weights = product[:, :width] + product[:, width : 2 * width] + product[:, 2 * width :]
    weights = jnp.concatenate([weights, jnp.zeros_like(weights)], axis=1).reshape(chips, SMALL, 2 * width)
    bias = jnp.sum(rows_grad, axis=0, keepdims=True)
    bias = jnp.concatenate([bias, jnp.zeros_like(bias)], axis=1)[None]
    sub = lax.broadcasted_iota(jnp.int32, weights.shape, 1)
    for c in range(2):
        own = weights if c == 0 else pltpu.roll(weights, 4, 1)
        small_ref[:, c] = jnp.where(sub < 4, own, jnp.where(sub == 4, bias, 0.0))

    batch = 16
    rows = big + SMALL
    row = lax.broadcasted_iota(jnp.int32, (batch, rows, 128), 1)
    diag = row == lax.broadcasted_iota(jnp.int32, (batch, rows, 128), 2)
    for i in range(0, chips, batch // 2):
        part = slice(i, i + batch // 2)
        parts = [keep_ref[v, part] + recv_ref[v, part] for v in range(tiles)] + [small_ref[part]]
        x = jnp.concatenate([p.reshape(batch, 8, 128) for p in parts], axis=1)
        q, power = to_levels(x)
        powers = jnp.sum(jnp.where(diag, power, 0.0), axis=1, keepdims=True)
        q = jnp.where(row == rows - 1, powers, q)
        out_ref[2 * i : 2 * i + batch] = q.astype(jnp.int32).astype(jnp.int16)


def last_kernel(z_ref, own_ref, partner_ref, enc_ref, pred_ref, encw_ref, predw_ref, outw_ref, bias_ref):
    core = lax.axis_index("batch")
    first = core == 0
    frame = lax.axis_index("frame")
    rows = z_ref.shape[1]
    big = rows - SMALL
    n = 8
    width = own_ref.shape[1] // 2
    total = [jnp.zeros((big, 128), F32)] * 2
    by_token = [jnp.zeros((SMALL, 128), F32)] * n
    by_frame = [jnp.zeros((SMALL, 128), F32)] * n
    for f in range(n):
        for k in range(n):
            for c in range(2):
                x = z_ref[(f * n + k) * 2 + c].astype(jnp.int32).astype(F32)
                x = from_levels(x, x[rows - 1 :])
                total[c] = total[c] + x[:big]
                if c == 0:
                    by_token[k] = by_token[k] + x[big:]
                else:
                    by_frame[f] = by_frame[f] + x[big:]
    for c in range(2):
        for t in range(big // 4):
            v = c * (big // 4) + t
            outw_ref[:, v * 128 : (v + 1) * 128] = total[c][t * 4 : t * 4 + 4, :]
    bias = jnp.zeros((1, 128), F32)
    for j in range(n):
        cols = slice(j * width, (j + 1) * width)
        encw_ref[:, cols] = by_token[j][:4, :width]
        predw_ref[:, cols] = by_frame[j][:4, :width]
        bias = bias + jnp.where(frame == j, by_token[j][4:5], 0.0)
    offset = lax.axis_index("token") * 8 + core * 4
    bias_ref[...] = pltpu.roll(bias, 128 - offset, 1)[:, :4]
    nt = enc_ref.shape[1]
    own, other = own_ref[:nt, :width], partner_ref[nt:, :width]
    enc_ref[0] = jnp.where(first, own, other)
    pred_ref[0] = jnp.where(first, other, own)


VM = pl.BlockSpec(memory_space=pltpu.VMEM)


def shape(*dims):
    return jax.ShapeDtypeStruct(dims, F32)


def local(
    encoder_out, predictor_out, enc_weight, pred_weight, joint_bias, out_weight,
    blank_occupancy, label_occupancy, frame_lengths, token_lengths, target_ids,
):
    joint, vocab = out_weight.shape
    nf, nt = blank_occupancy.shape[1:]
    width = encoder_out.shape[2]
    core = lax.axis_index("batch")
    n = lax.axis_size("frame")
    groups = [[f * 2 * n + k * 2 for k in range(n)] for f in range(n)]
    groups += [[f * 2 * n + k * 2 + 1 for f in range(n)] for k in range(n)]

    def swap(x):
        return lax.ppermute(x, "batch", [(0, 1), (1, 0)])

    def exchange(x):
        return lax.all_to_all(x, ALL, 0, 0, axis_index_groups=groups)

    enc, pred = encoder_out[0], predictor_out[0]
    def spread(own, other):
        return jnp.broadcast_to(jnp.where(core == 0, own, other)[None], (n, nf, width))

    payload = jnp.concatenate([spread(enc, pred), spread(swap(enc), swap(pred))], axis=2)
    (
        payload, enc_weight, pred_weight, out_weight, blank_occupancy, label_occupancy, joint_bias, target_ids,
        frame_lengths, token_lengths,
    ) = lax.optimization_barrier((
        payload, enc_weight, pred_weight, out_weight, blank_occupancy, label_occupancy, joint_bias, target_ids,
        frame_lengths, token_lengths,
    ))
    gathered = exchange(payload)

    cells = nf * nt
    lengths = jnp.concatenate([frame_lengths, token_lengths])
    per_cell = jnp.concatenate(
        [
            jnp.concatenate([blank_occupancy[0], label_occupancy[0]], axis=1),
            joint_bias.reshape(joint // 128, 128),
            target_ids.astype(F32).reshape(1, 2 * nt),
            jnp.pad(lengths.astype(F32)[None], ((0, 2), (0, 128 - lengths.shape[0]))),
        ],
        axis=0,
    )
    weights = jnp.concatenate([out_weight, enc_weight, pred_weight], axis=1)
    gathered, weights, per_cell = lax.optimization_barrier((gathered, weights, per_cell))
    partner = swap(gathered)
    tiles = vocab // 512
    term_keep, term_send, ow_keep, ow_send, features = pl.pallas_call(
        cells_kernel,
        out_shape=[
            jax.ShapeDtypeStruct((n, 2 * (nf + TAIL), 2 * width), jnp.int16),
            jax.ShapeDtypeStruct((n, nf + TAIL, 2 * width), jnp.int16),
        ]
        + [shape(tiles, joint // 8, 2, 8, 128)] * 2
        + [jax.ShapeDtypeStruct((joint, 2 * nt), BF16)],
        in_specs=[VM] * 4,
        out_specs=[VM] * 5,
        scratch_shapes=[
            pltpu.VMEM((nf, joint), F32),
            pltpu.VMEM((nt, joint), F32),
            pltpu.VMEM((nf, joint), F32),
            pltpu.VMEM((nt, joint), F32),
            pltpu.VMEM((nt, 128), jnp.int32),
            pltpu.VMEM((nf, 2 * nt), F32),
            pltpu.VMEM((FB * nt, vocab), F32),
            pltpu.VMEM((cells, joint + vocab), BF16),
        ],
        compiler_params=pltpu.CompilerParams(vmem_limit_bytes=40 * 1024 * 1024),
        name="joint_cells",
    )(gathered, partner, weights, per_cell)

    term_recv, ow_send = lax.optimization_barrier((swap(term_send), ow_send))
    ow_recv = swap(ow_send)
    sums = lax.dynamic_update_slice(term_keep, term_recv, (0, nf + TAIL, 0))
    summed = exchange(sums)
    own = pl.pallas_call(
        sum_kernel,
        out_shape=shape(2 * nf, 2 * width),
        in_specs=[VM],
        out_specs=VM,
        compiler_params=pltpu.CompilerParams(vmem_limit_bytes=16 * 1024 * 1024),
        name="sum_rows",
    )(summed)
    partner_own = swap(own)
    payload = pl.pallas_call(
        pack_kernel,
        out_shape=jax.ShapeDtypeStruct((joint // 4, tiles * 8 + SMALL, 128), jnp.int16),
        in_specs=[VM] * 4,
        out_specs=VM,
        scratch_shapes=[pltpu.VMEM((joint // 8, 2, SMALL, 2 * width), F32)],
        compiler_params=pltpu.CompilerParams(vmem_limit_bytes=16 * 1024 * 1024),
        name="pack_shares",
    )(ow_keep, ow_recv, own, features)
    payload, partner_own = lax.optimization_barrier((payload, partner_own))
    shares = lax.all_to_all(payload, ALL, 0, 0)
    own_rows = joint // 128
    enc_grad, pred_grad, enc_wgrad, pred_wgrad, out_wgrad, bias_grad = pl.pallas_call(
        last_kernel,
        out_shape=[
            shape(1, nf, width), shape(1, nt, width), shape(own_rows, joint), shape(own_rows, joint),
            shape(own_rows, vocab), shape(1, own_rows),
        ],
        in_specs=[VM] * 3,
        out_specs=[VM] * 6,
        compiler_params=pltpu.CompilerParams(vmem_limit_bytes=24 * 1024 * 1024),
        name="sum_shares",
    )(shares, own, partner_own)
    return enc_grad, pred_grad, enc_wgrad, pred_wgrad, out_wgrad, bias_grad[0]


def solution(mesh):
    in_specs = (
        P("batch", "frame", "token"),
        P("batch", "token", "frame"),
        P(),
        P(),
        P(),
        P(),
        P("batch", "frame", "token"),
        P("batch", "frame", "token"),
        P(),
        P(),
        P(None, "token"),
    )
    out_specs = (
        P("batch", "frame", "token"),
        P("batch", "token", "frame"),
        P(ALL, None),
        P(ALL, None),
        P(ALL, None),
        P(ALL),
    )
    return jax.shard_map(local, mesh=mesh, in_specs=in_specs, out_specs=out_specs, check_vma=False)
```

```python
import jax
import jax.numpy as jnp
from jax import lax
from jax.experimental import pallas as pl
from jax.experimental.pallas import tpu as pltpu
from jax.sharding import PartitionSpec as P

FB = 16
CHUNK = 256
LEVELS = 32000.0
STEPS = 16.0
SMALL = 8
TAIL = 16
ALL = ("frame", "token", "batch")
F32, BF16 = jnp.float32, jnp.bfloat16


def split3(x):
    hi = x.astype(BF16)
    rest = x - hi.astype(F32)
    mid = rest.astype(BF16)
    lo = (rest - mid.astype(F32)).astype(BF16)
    return hi, mid, lo


def dot_nt(a, b):
    return lax.dot_general(a, b, (((1,), (1,)), ((), ())), preferred_element_type=F32)


def dot_tn(a, b):
    return lax.dot_general(a, b, (((0,), (0,)), ((), ())), preferred_element_type=F32)


def exact_nt(a, b):
    rows = a.shape[0]
    product = dot_nt(jnp.concatenate(split3(a), axis=0), b)
    return product[:rows] + product[rows : 2 * rows] + product[2 * rows :]


def to_levels(x):
    largest = jnp.maximum(jnp.max(jnp.abs(x), axis=-1, keepdims=True), 1e-30)
    power = jnp.ceil(jnp.log2(largest) * STEPS)
    return jnp.round(x * (LEVELS * jnp.exp2(power * (-1.0 / STEPS)))), power


def from_levels(x, powers):
    rows = x.shape[0]
    diag = lax.broadcasted_iota(jnp.int32, (rows, 128), 0) == lax.broadcasted_iota(jnp.int32, (rows, 128), 1)
    power = jnp.sum(jnp.where(diag, powers, 0.0), axis=1, keepdims=True)
    return x * (jnp.exp2(power * (1.0 / STEPS)) * (1.0 / LEVELS))


def halves(ref, first_half):
    width = ref.shape[2] // 2
    start = 0 if first_half else width
    pieces = [ref[s].astype(F32)[:, start : start + width] for s in range(ref.shape[0])]
    return jnp.concatenate(pieces, axis=1).astype(BF16)


def exact_tn(a, b):
    return sum(dot_tn(a, piece) for piece in split3(b))


def cells_kernel(
    g_ref, h_ref, weights_ref, cell_ref, keep_ref, send_ref, ow_keep_ref, ow_send_ref,
    encp_ref, predp_ref, rows_ref, prow_ref, tgt_col_ref, occ_ref, e_ref, stash_ref,
):
    nf, nt = encp_ref.shape[0], predp_ref.shape[0]
    joint, vocab = encp_ref.shape[1], e_ref.shape[1]
    ow_ref = weights_ref.at[:, :vocab]
    encw_ref = weights_ref.at[:, vocab : vocab + joint]
    predw_ref = weights_ref.at[:, vocab + joint :]
    parts, width = g_ref.shape[0], g_ref.shape[2] // 2
    cells = FB * nt
    first = lax.axis_index("batch") == 0
    own, other = halves(g_ref, True), halves(h_ref, False)
    encp_ref[...] = jnp.dot(jnp.where(first, own, other), encw_ref[...], preferred_element_type=F32)
    predp = jnp.dot(jnp.where(first, other, own), predw_ref[...], preferred_element_type=F32)
    for v in range(joint // 128):
        cols = slice(v * 128, (v + 1) * 128)
        predp_ref[:, cols] = predp[:, cols] + cell_ref[nf + v : nf + v + 1, :]
    diag_row = lax.broadcasted_iota(jnp.int32, (nt, 128), 0)
    diag_lane = lax.broadcasted_iota(jnp.int32, (nt, 128), 1)
    blank_diag, label_diag = diag_row == diag_lane, diag_row + nt == diag_lane
    core = lax.axis_index("batch")
    row = nf + joint // 128
    mine = diag_row + nt * core == diag_lane
    targets = jnp.sum(jnp.where(mine, cell_ref[row : row + 1, :], 0.0), axis=1, keepdims=True)
    tgt_col_ref[...] = jnp.broadcast_to(targets.astype(jnp.int32), (nt, 128))
    lengths = cell_ref[row + 1 : row + 2, :]
    lane1 = diag_lane[:1]
    frame_len = jnp.sum(jnp.where(lane1 == core, lengths, 0.0), axis=1, keepdims=True).astype(jnp.int32)
    token_len = jnp.sum(jnp.where(lane1 == core + 2, lengths, 0.0), axis=1, keepdims=True).astype(jnp.int32)
    frame_pos = lax.axis_index("frame") * nf + lax.broadcasted_iota(jnp.int32, (nf, 128), 0)
    token_pos = lax.axis_index("token") * nt + lax.rem(lax.broadcasted_iota(jnp.int32, (nf, 128), 1), nt)
    reach = jnp.where(lax.broadcasted_iota(jnp.int32, (nf, 128), 1) < nt, token_len, token_len - 1)
    occ_ref[...] = jnp.where((frame_pos < frame_len) & (token_pos <= reach), cell_ref[:nf, :], 0.0)
    prow_ref[...] = jnp.zeros_like(prow_ref)
    lane = lax.broadcasted_iota(jnp.int32, (FB, nt, 128), 2)

    def columns(diag, t0):
        rows = occ_ref[pl.ds(t0, FB), :]
        return jnp.sum(jnp.where(diag[None], rows[:, None, :], 0.0), axis=2, keepdims=True)

    def block(i, carry):
        t0 = pl.multiple_of(i * FB, FB)
        span = pl.ds(pl.multiple_of(i * cells, cells), cells)
        frames = encp_ref[pl.ds(t0, FB), :]
        inner = frames[:, None, :] + predp_ref[...][None, :, :]
        hidden = jnp.tanh(inner).astype(BF16).reshape(cells, joint)
        stash_ref[span, :joint] = hidden
        total = jnp.zeros((cells, 128), F32)
        for c in range(vocab // CHUNK):
            cols = slice(c * CHUNK, (c + 1) * CHUNK)
            e = jnp.exp(jnp.dot(hidden, ow_ref[:, cols], preferred_element_type=F32))
            e_ref[:, cols] = e
            for q in range(CHUNK // 128):
                total = total + e[:, q * 128 : (q + 1) * 128]
        total = jnp.sum(total, axis=1, keepdims=True).reshape(FB, nt, 1)
        bw = columns(blank_diag, t0)
        lw = columns(label_diag, t0)
        scale = (bw + lw) / total
        tgt = tgt_col_ref[...][None]
        for v in range(vocab // 128):
            cols = slice(v * 128, (v + 1) * 128)
            g = e_ref[:, cols].reshape(FB, nt, 128) * scale
            if v == 0:
                g = g - jnp.where(lane == 0, bw, 0.0)
            g = g - jnp.where(lane == tgt - v * 128, lw, 0.0)
            stash_ref[span, joint + v * 128 : joint + (v + 1) * 128] = g.astype(BF16).reshape(cells, 128)
        for c in range(joint // CHUNK):
            cols = slice(c * CHUNK, (c + 1) * CHUNK)
            grad_hidden = dot_nt(stash_ref[span, joint:], ow_ref[cols, :])
            hf = stash_ref[span, cols].astype(F32)
            gi = (grad_hidden * (1.0 - hf * hf)).reshape(FB, nt, CHUNK)
            prow_ref[:, cols] += gi.sum(0)
            rows_ref[pl.ds(t0, FB), cols] = gi.sum(1)
        return carry

    lax.fori_loop(0, nf // FB, block, 0)

    term_e = exact_nt(rows_ref[...], encw_ref[...])
    term_p = exact_nt(prow_ref[...], predw_ref[...])
    for s in range(parts):
        cols = slice(s * width, (s + 1) * width)
        e_part = jnp.concatenate([term_e[:, cols], rows_ref[:, cols]], axis=1)
        p_part = jnp.concatenate([term_p[:, cols], prow_ref[:, cols]], axis=1)
        for ref, part in ((keep_ref, jnp.where(first, e_part, p_part)), (send_ref, jnp.where(first, p_part, e_part))):
            q, power = to_levels(part)
            powers = jnp.sum(jnp.where(blank_diag, power, 0.0), axis=0, keepdims=True)
            q = jnp.concatenate([q, jnp.broadcast_to(powers, (TAIL, 128))], axis=0)
            ref[s, : nt + TAIL, :] = q.astype(jnp.int32).astype(jnp.int16)

    chips = joint // 8
    top = lax.broadcasted_iota(jnp.int32, (chips, 8, 128), 1) < 4
    half = vocab // 2
    for dest_ref, part in ((ow_send_ref, 1 - core), (ow_keep_ref, core)):
        start = pl.multiple_of(joint + part * half, 128)
        acc = dot_tn(stash_ref[:, :joint], stash_ref[:, pl.ds(start, half)])
        for v in range(half // 256):
            a = acc[:, v * 256 : v * 256 + 128].reshape(chips, 8, 128)
            b = acc[:, v * 256 + 128 : v * 256 + 256].reshape(chips, 8, 128)
            dest_ref[v, :, 0] = jnp.where(top, a, pltpu.roll(b, 4, 1))
            dest_ref[v, :, 1] = jnp.where(top, pltpu.roll(a, 4, 1), b)


def features_kernel(g_ref, feat_ref):
    parts = [halves(g_ref, side).astype(F32).T for side in (True, False)]
    feat_ref[...] = jnp.concatenate(parts, axis=1).astype(BF16)


def sum_kernel(y_ref, total_ref):
    span = y_ref.shape[1] // 2
    nt = span - TAIL
    for h in range(2):
        total = jnp.zeros((nt, y_ref.shape[2]), F32)
        for s in range(y_ref.shape[0]):
            x = y_ref[s, h * span : (h + 1) * span, :].astype(jnp.int32).astype(F32)
            total = total + from_levels(x[:nt], x[nt : nt + 1])
        total_ref[h * nt : (h + 1) * nt, :] = total


def pack_kernel(keep_ref, recv_ref, total_ref, feat_ref, out_ref, small_ref):
    tiles, chips = keep_ref.shape[:2]
    big = tiles * 8
    total = total_ref[...]
    width = total.shape[1] // 2
    rows_grad = total[:, width:]
    pieces = jnp.concatenate(split3(rows_grad), axis=1)
    product = jnp.dot(feat_ref[...], pieces, preferred_element_type=F32)
    weights = product[:, :width] + product[:, width : 2 * width] + product[:, 2 * width :]
    weights = jnp.concatenate([weights, jnp.zeros_like(weights)], axis=1).reshape(chips, SMALL, 2 * width)
    bias = jnp.sum(rows_grad, axis=0, keepdims=True)
    bias = jnp.concatenate([bias, jnp.zeros_like(bias)], axis=1)[None]
    sub = lax.broadcasted_iota(jnp.int32, weights.shape, 1)
    for c in range(2):
        own = weights if c == 0 else pltpu.roll(weights, 4, 1)
        small_ref[:, c] = jnp.where(sub < 4, own, jnp.where(sub == 4, bias, 0.0))

    batch = 16
    rows = big + SMALL
    row = lax.broadcasted_iota(jnp.int32, (batch, rows, 128), 1)
    diag = row == lax.broadcasted_iota(jnp.int32, (batch, rows, 128), 2)
    for i in range(0, chips, batch // 2):
        part = slice(i, i + batch // 2)
        parts = [keep_ref[v, part] + recv_ref[v, part] for v in range(tiles)] + [small_ref[part]]
        x = jnp.concatenate([p.reshape(batch, 8, 128) for p in parts], axis=1)
        q, power = to_levels(x)
        powers = jnp.sum(jnp.where(diag, power, 0.0), axis=1, keepdims=True)
        q = jnp.where(row == rows - 1, powers, q)
        out_ref[2 * i : 2 * i + batch] = q.astype(jnp.int32).astype(jnp.int16)


def last_kernel(z_ref, own_ref, partner_ref, enc_ref, pred_ref, encw_ref, predw_ref, outw_ref, bias_ref):
    core = lax.axis_index("batch")
    first = core == 0
    frame = lax.axis_index("frame")
    rows = z_ref.shape[1]
    big = rows - SMALL
    n = 8
    width = own_ref.shape[1] // 2
    total = [jnp.zeros((big, 128), F32)] * 2
    by_token = [jnp.zeros((SMALL, 128), F32)] * n
    by_frame = [jnp.zeros((SMALL, 128), F32)] * n
    for f in range(n):
        for k in range(n):
            for c in range(2):
                x = z_ref[(f * n + k) * 2 + c].astype(jnp.int32).astype(F32)
                x = from_levels(x, x[rows - 1 :])
                total[c] = total[c] + x[:big]
                if c == 0:
                    by_token[k] = by_token[k] + x[big:]
                else:
                    by_frame[f] = by_frame[f] + x[big:]
    for c in range(2):
        for t in range(big // 4):
            v = c * (big // 4) + t
            outw_ref[:, v * 128 : (v + 1) * 128] = total[c][t * 4 : t * 4 + 4, :]
    bias = jnp.zeros((1, 128), F32)
    for j in range(n):
        cols = slice(j * width, (j + 1) * width)
        encw_ref[:, cols] = by_token[j][:4, :width]
        predw_ref[:, cols] = by_frame[j][:4, :width]
        bias = bias + jnp.where(frame == j, by_token[j][4:5], 0.0)
    offset = lax.axis_index("token") * 8 + core * 4
    bias_ref[...] = pltpu.roll(bias, 128 - offset, 1)[:, :4]
    nt = enc_ref.shape[1]
    own, other = own_ref[:nt, :width], partner_ref[nt:, :width]
    enc_ref[0] = jnp.where(first, own, other)
    pred_ref[0] = jnp.where(first, other, own)


VM = pl.BlockSpec(memory_space=pltpu.VMEM)


def shape(*dims):
    return jax.ShapeDtypeStruct(dims, F32)


def local(
    encoder_out, predictor_out, enc_weight, pred_weight, joint_bias, out_weight,
    blank_occupancy, label_occupancy, frame_lengths, token_lengths, target_ids,
):
    joint, vocab = out_weight.shape
    nf, nt = blank_occupancy.shape[1:]
    width = encoder_out.shape[2]
    core = lax.axis_index("batch")
    n = lax.axis_size("frame")
    groups = [[f * 2 * n + k * 2 for k in range(n)] for f in range(n)]
    groups += [[f * 2 * n + k * 2 + 1 for f in range(n)] for k in range(n)]

    def swap(x):
        return lax.ppermute(x, "batch", [(0, 1), (1, 0)])

    def exchange(x):
        return lax.all_to_all(x, ALL, 0, 0, axis_index_groups=groups)

    enc, pred = encoder_out[0], predictor_out[0]
    def spread(own, other):
        return jnp.broadcast_to(jnp.where(core == 0, own, other)[None], (n, nf, width))

    payload = jnp.concatenate([spread(enc, pred), spread(swap(enc), swap(pred))], axis=2)
    (
        payload, enc_weight, pred_weight, out_weight, blank_occupancy, label_occupancy, joint_bias, target_ids,
        frame_lengths, token_lengths,
    ) = lax.optimization_barrier((
        payload, enc_weight, pred_weight, out_weight, blank_occupancy, label_occupancy, joint_bias, target_ids,
        frame_lengths, token_lengths,
    ))
    gathered = exchange(payload)

    cells = nf * nt
    lengths = jnp.concatenate([frame_lengths, token_lengths])
    per_cell = jnp.concatenate(
        [
            jnp.concatenate([blank_occupancy[0], label_occupancy[0]], axis=1),
            joint_bias.reshape(joint // 128, 128),
            target_ids.astype(F32).reshape(1, 2 * nt),
            jnp.pad(lengths.astype(F32)[None], ((0, 2), (0, 128 - lengths.shape[0]))),
        ],
        axis=0,
    )
    weights = jnp.concatenate([out_weight, enc_weight, pred_weight], axis=1)
    gathered, weights, per_cell = lax.optimization_barrier((gathered, weights, per_cell))
    partner = swap(gathered)
    tiles = vocab // 512
    features = pl.pallas_call(
        features_kernel,
        out_shape=jax.ShapeDtypeStruct((joint, 2 * nt), BF16),
        in_specs=[VM],
        out_specs=VM,
        compiler_params=pltpu.CompilerParams(vmem_limit_bytes=16 * 1024 * 1024),
        name="features",
    )(gathered)
    term_keep, term_send, ow_keep, ow_send = pl.pallas_call(
        cells_kernel,
        out_shape=[
            jax.ShapeDtypeStruct((n, 2 * (nf + TAIL), 2 * width), jnp.int16),
            jax.ShapeDtypeStruct((n, nf + TAIL, 2 * width), jnp.int16),
        ]
        + [shape(tiles, joint // 8, 2, 8, 128)] * 2,
        in_specs=[VM] * 4,
        out_specs=[VM] * 4,
        scratch_shapes=[
            pltpu.VMEM((nf, joint), F32),
            pltpu.VMEM((nt, joint), F32),
            pltpu.VMEM((nf, joint), F32),
            pltpu.VMEM((nt, joint), F32),
            pltpu.VMEM((nt, 128), jnp.int32),
            pltpu.VMEM((nf, 2 * nt), F32),
            pltpu.VMEM((FB * nt, vocab), F32),
            pltpu.VMEM((cells, joint + vocab), BF16),
        ],
        compiler_params=pltpu.CompilerParams(vmem_limit_bytes=40 * 1024 * 1024),
        name="joint_cells",
    )(gathered, partner, weights, per_cell)

    term_recv, ow_send = lax.optimization_barrier((swap(term_send), ow_send))
    ow_recv = swap(ow_send)
    sums = lax.dynamic_update_slice(term_keep, term_recv, (0, nf + TAIL, 0))
    summed = exchange(sums)
    own = pl.pallas_call(
        sum_kernel,
        out_shape=shape(2 * nf, 2 * width),
        in_specs=[VM],
        out_specs=VM,
        compiler_params=pltpu.CompilerParams(vmem_limit_bytes=16 * 1024 * 1024),
        name="sum_rows",
    )(summed)
    partner_own = swap(own)
    payload = pl.pallas_call(
        pack_kernel,
        out_shape=jax.ShapeDtypeStruct((joint // 4, tiles * 8 + SMALL, 128), jnp.int16),
        in_specs=[VM] * 4,
        out_specs=VM,
        scratch_shapes=[pltpu.VMEM((joint // 8, 2, SMALL, 2 * width), F32)],
        compiler_params=pltpu.CompilerParams(vmem_limit_bytes=16 * 1024 * 1024),
        name="pack_shares",
    )(ow_keep, ow_recv, own, features)
    payload, partner_own = lax.optimization_barrier((payload, partner_own))
    shares = lax.all_to_all(payload, ALL, 0, 0)
    own_rows = joint // 128
    enc_grad, pred_grad, enc_wgrad, pred_wgrad, out_wgrad, bias_grad = pl.pallas_call(
        last_kernel,
        out_shape=[
            shape(1, nf, width), shape(1, nt, width), shape(own_rows, joint), shape(own_rows, joint),
            shape(own_rows, vocab), shape(1, own_rows),
        ],
        in_specs=[VM] * 3,
        out_specs=[VM] * 6,
        compiler_params=pltpu.CompilerParams(vmem_limit_bytes=24 * 1024 * 1024),
        name="sum_shares",
    )(shares, own, partner_own)
    return enc_grad, pred_grad, enc_wgrad, pred_wgrad, out_wgrad, bias_grad[0]


def solution(mesh):
    in_specs = (
        P("batch", "frame", "token"),
        P("batch", "token", "frame"),
        P(),
        P(),
        P(),
        P(),
        P("batch", "frame", "token"),
        P("batch", "frame", "token"),
        P(),
        P(),
        P(None, "token"),
    )
    out_specs = (
        P("batch", "frame", "token"),
        P("batch", "token", "frame"),
        P(ALL, None),
        P(ALL, None),
        P(ALL, None),
        P(ALL),
    )
    return jax.shard_map(local, mesh=mesh, in_specs=in_specs, out_specs=out_specs, check_vma=False)
```
